32 devices in a mesh: tm: 4 (over z), sx: 2 (over y), sy: 4 (over x, core).
Axes of the slice: x: 2, y: 2, z: 4, core: 2. Of those that a mesh axis runs over, the one named last changes fastest.
Arguments:
- wall_temp: bfloat16 [64, 8192, 128], P('tm', ('sx', 'sy')), may hold values from -6 to 6
- owner_map: int32 [8192, 1], P(('sx', 'sy')), may hold values from 0 to 7; in each aligned block of 1024 rows (0 to 1023, 1024 to 2047, ...) at most 256 rows name the same one
- stencil_column: int32 [8192], P(('sx', 'sy')), may hold values from 0 to 255
- material: int32 [32, 64, 128], P('sx', 'sy'), may hold values from 0 to 3
- conductivity: float32 [4], replicated, may hold values from 0.1 to 1
- capacity: float32 [4], replicated, may hold values from 0.2 to 1
Outputs:
- temperature: float32 [32, 2, 32, 64, 128], P('tm', None, 'sx', 'sy')
The draws below stay inside these ranges and needn't reach their ends.
Inputs may be any that keep to these rules, and one draw needn't show every extreme that they name: `owner_map`: among the 1024 patches of one device (aligned blocks of rows), no owner is named more than 256 times, a bound that some block reaches.
All inputs are finite; a program needn't handle non-finite values.
Results may differ from the reference program's by a relative error of at most 0.0034.
Values may be sent and summed in bfloat16 or wider, within the bound.
A program may use at most 64 MiB of HBM per device.

```python
import math
import jax
import jax.numpy as jnp
import numpy as np
from jax import lax

TIME = 64
HARM = 32
PW = 128
NMAT = 4
SWEEPS = 4
PATCH_DEV = 1024
BX = 16
BY = 16
OWNERS = 8
CAP = 256
PATCHES = 8192
NX = 32
NY = 64
N_SY = 4


def with_ends(result, stream_key, smallest, top_value):
    place = [jax.random.randint(jax.random.fold_in(stream_key, axis), (), 0, length) for axis, length in enumerate(result.shape)]
    longest = result.shape.index(max(result.shape))
    neighbour = place[:longest] + [(place[longest] + 1) % result.shape[longest]] + place[longest + 1:]
    return result.at[tuple(place)].set(smallest).at[tuple(neighbour)].set(top_value)


def shard_levels(stream_key, shape, cuts, least, top_value):
    def one(dim, parts):
        draws = jax.random.uniform(jax.random.fold_in(jax.random.fold_in(stream_key, 6), dim), (parts,), jnp.float32, least / len(cuts), top_value / len(cuts))
        return jnp.repeat(jnp.exp(draws), shape[dim] // parts).reshape((-1,) + (1,) * (len(shape) - dim - 1))

    gain = one(*cuts[0])
    for cut in cuts[1:]:
        gain = gain * one(*cut)
    return gain


def routed_block(own_key, own, number, rows, count, top, most, skew):
    order = jax.random.permutation(own_key, count)
    crowded, usual = load_shares(count, rows * top, most, skew, True), load_shares(count, rows * top, most, skew, False)
    places = jnp.arange(count)

    def named(tallies, turn):
        used = int((tallies > 0).sum())
        fixed = max(1, used // 4)
        moved = fixed + (places - fixed + turn * (used - fixed)) % max(1, count - fixed)
        return jnp.zeros((count,), jnp.int32).at[order[jnp.where(places < fixed, places, moved)]].set(jnp.asarray(tallies, jnp.int32))

    tallies = jnp.where(number % 4 == 0, named(crowded, number // 4), named(usual, number - number // 4 - 1))
    mixed = jax.random.permutation(jax.random.fold_in(own, 3), count)
    giver, receiver = mixed[0:count // 2 * 2:2], mixed[1:count // 2 * 2:2]
    slack = jnp.minimum(tallies[giver] - 1, most - tallies[receiver]) // 2
    slack = jnp.where((giver == order[0]) | (receiver == order[0]) | (tallies[receiver] == 0), 0, jnp.maximum(slack, 0))
    moved = jax.random.randint(jax.random.fold_in(own, 4), (count // 2,), 0, 1 << 20) % (slack + 1)
    tallies = tallies.at[giver].add(-moved).at[receiver].add(moved)
    items = jnp.searchsorted(jnp.cumsum(tallies), jnp.arange(rows * top), side="right").astype(jnp.int32)
    listing = items.reshape(top, rows).T
    listing = listing[jax.random.permutation(jax.random.fold_in(own, 1), rows)]
    turn = jax.random.randint(jax.random.fold_in(own, 2), (rows, 1), 0, top)
    return jnp.take_along_axis(listing, (jnp.arange(top)[None, :] + turn) % top, axis=1)


def load_shares(number_of, total, reach, slope, full):
    portions = [(1 << 20) // math.isqrt(standing ** slope) + 1 for standing in range(1, number_of + 1)]
    largest = reach if full else min(reach, max(-(-total // number_of), total * portions[0] // sum(portions)))
    least = 1 if total - largest >= number_of - 1 else 0
    holding, surplus = [largest] + [least] * (number_of - 1), total - largest - least * (number_of - 1)
    while surplus > 0:
        movable = [i for i in range(1, number_of) if holding[i] < largest] or [i for i in range(1, number_of) if holding[i] < reach]
        mass, remaining = sum([portions[i] for i in movable]), surplus
        for i in movable:
            extra = min(reach - holding[i], max(1, remaining * portions[i] // mass), surplus)
            holding[i] = holding[i] + extra
            surplus = surplus - extra
    return np.array(holding)


def noise(stream_key, extent, spread, most, shards=(), kind=jnp.bfloat16):
    result = spread * jax.random.normal(stream_key, extent, jnp.float32)
    if shards:
        result = result * shard_levels(stream_key, extent, shards, -0.22, 0.18)
    return jnp.clip(result, -most, most).astype(kind)


def setup_inputs(seed: int = 0) -> dict:
    keys = jax.random.split(jax.random.key(seed), 7)
    wall_temp = noise(keys[0], (TIME, PATCHES, PW), 1.0, 6.0, ((0, 4), (1, 8)))
    owner_map_keys = jax.random.split(jax.random.fold_in(keys[1], 1), PATCHES // PATCH_DEV)
    owner_map_turns = jax.random.permutation(jax.random.fold_in(keys[1], 3), PATCHES // PATCH_DEV)
    owner_map = jax.vmap(lambda own, number: routed_block(jax.random.fold_in(keys[1], 2), own, number, PATCH_DEV, OWNERS, 1, CAP, 2))(owner_map_keys, owner_map_turns).reshape((PATCHES, 1))
    stencil_column = with_ends(jax.random.randint(keys[2], (PATCHES,), 0, BX * BY), jax.random.fold_in(keys[2], 1), 0, (BX * BY) - 1).astype(jnp.int32)
    material = with_ends(jax.random.randint(keys[3], (NX, NY, PW), 0, NMAT), jax.random.fold_in(keys[3], 1), 0, NMAT - 1).astype(jnp.int32)
    conductivity = jnp.clip(jnp.exp(jax.random.uniform(keys[4], (NMAT,), jnp.float32, math.log(0.1), math.log(1.0))), 0.1, 1.0)
    capacity = jnp.clip(jnp.exp(jax.random.uniform(keys[5], (NMAT,), jnp.float32, math.log(0.2), math.log(1.0))), 0.2, 1.0)
    return {"wall_temp": wall_temp, "owner_map": owner_map, "stencil_column": stencil_column, "material": material, "conductivity": conductivity, "capacity": capacity}


omega_step = 0.1

def dft_table():
    freq_index = jnp.arange(HARM, dtype=jnp.int32)
    time_index = jnp.arange(TIME, dtype=jnp.int32)
    phase_int = freq_index[:, None] * time_index[None, :] % TIME
    angles = phase_int.astype(jnp.float32) * jnp.float32(2.0 * math.pi / TIME)
    amplitude = jnp.float32(2.0 / math.sqrt(TIME))
    table_rows = jnp.stack([amplitude * jnp.cos(angles), -amplitude * jnp.sin(angles)], axis=1)
    return table_rows.reshape(2 * HARM, TIME).astype(jnp.bfloat16)

def lookup(material, table):
    values = jnp.zeros(material.shape, jnp.float32)
    for material_id in range(NMAT):
        values = jnp.where(material == material_id, table[material_id], values)
    return values

def face_value(conduct, other):
    other = jnp.where(other > 0, other, conduct)
    return 2.0 * conduct * other / (conduct + other)

def face_values(conduct, padded):
    next_x = face_value(conduct, padded[2:, 1:-1, 1:-1])
    prev_x = face_value(conduct, padded[:-2, 1:-1, 1:-1])
    next_y = face_value(conduct, padded[1:-1, 2:, 1:-1])
    prev_y = face_value(conduct, padded[1:-1, :-2, 1:-1])
    next_z = face_value(conduct, padded[1:-1, 1:-1, 2:])
    prev_z = face_value(conduct, padded[1:-1, 1:-1, :-2])
    total = next_x + prev_x + next_y + prev_y + next_z + prev_z
    return ((next_x, prev_x, next_y, prev_y, next_z, prev_z), total)

def relax_sweep(padded, source, faces, real_den, imag_den):
    next_x, prev_x, next_y, prev_y, next_z, prev_z = faces
    nearby = next_x * padded[..., 2:, 1:-1, 1:-1] + prev_x * padded[..., :-2, 1:-1, 1:-1]
    nearby = nearby + next_y * padded[..., 1:-1, 2:, 1:-1] + prev_y * padded[..., 1:-1, :-2, 1:-1]
    nearby = nearby + next_z * padded[..., 1:-1, 1:-1, 2:] + prev_z * padded[..., 1:-1, 1:-1, :-2]
    numerator = source + nearby
    real_num = numerator[..., 0, :, :, :]
    imag_num = numerator[..., 1, :, :, :]
    modulus = real_den * real_den + imag_den * imag_den
    real_out = (real_num * real_den + imag_num * imag_den) / modulus
    imag_out = (imag_num * real_den - real_num * imag_den) / modulus
    return jnp.stack([real_out, imag_out], axis=-4)

def reference(wall_temp, owner_map, stencil_column, material, conductivity, capacity):
    transform_rows = dft_table()
    flattened = wall_temp.reshape(TIME, PATCHES * PW)
    harmonic = jnp.dot(transform_rows, flattened, preferred_element_type=jnp.float32)
    harmonic = harmonic.astype(jnp.bfloat16).reshape(2 * HARM, PATCHES, PW)
    owner_ids = owner_map[:, 0]
    cell_x = owner_ids // N_SY * BX + stencil_column // BY
    cell_y = owner_ids % N_SY * BY + stencil_column % BY
    target = (cell_x * NY + cell_y).astype(jnp.int32)
    conduct = lookup(material, conductivity)
    heat_cap = lookup(material, capacity)
    rim = jnp.pad(conduct, 1, mode='edge')
    faces, real_den = face_values(conduct, rim)

    def per_harmonic(index):
        pair = lax.dynamic_slice_in_dim(harmonic, 2 * index, 2, 0).astype(jnp.float32)
        summed = jax.ops.segment_sum(jnp.transpose(pair, (1, 0, 2)), target, NX * NY)
        source = jnp.transpose(summed.reshape(NX, NY, 2, PW), (2, 0, 1, 3))
        imag_den = omega_step * index.astype(jnp.float32) * heat_cap
        field = relax_sweep(jnp.zeros((2, NX + 2, NY + 2, PW + 2), jnp.float32), source, faces, real_den, imag_den)
        for sweep in range(SWEEPS - 1):
            padded = jnp.pad(field, ((0, 0), (1, 1), (1, 1), (1, 1)))
            field = relax_sweep(padded, source, faces, real_den, imag_den)
        return field
    return lax.map(per_harmonic, jnp.arange(HARM, dtype=jnp.int32))
```

```python
import functools
import math

import jax
import jax.numpy as jnp
from jax import lax
from jax.experimental import pallas as pl
from jax.experimental.pallas import tpu as pltpu
from jax.sharding import PartitionSpec as P

TIME = 64
HARM = 32
NMAT = 4
SWEEPS = 4


omega_step = 0.1


def with_halo(block, sides, width):
    for axis, dim in sides:
        count = lax.axis_size(axis)
        forward = [(i, i + 1) for i in range(count - 1)]
        backward = [(target, source) for source, target in forward]
        low = lax.ppermute(
            lax.slice_in_dim(block, block.shape[dim] - width, None, axis=dim), axis, forward
        )
        high = lax.ppermute(lax.slice_in_dim(block, 0, width, axis=dim), axis, backward)
        block = jnp.concatenate([low, block, high], axis=dim)
    return block


def dft_table():
    freq_index = jnp.arange(HARM, dtype=jnp.int32)
    time_index = jnp.arange(TIME, dtype=jnp.int32)
    phase_int = freq_index[:, None] * time_index[None, :] % TIME
    angles = phase_int.astype(jnp.float32) * jnp.float32(2.0 * math.pi / TIME)
    amplitude = jnp.float32(2.0 / math.sqrt(TIME))
    table_rows = jnp.stack([amplitude * jnp.cos(angles), -amplitude * jnp.sin(angles)], axis=1)
    return table_rows.reshape(2 * HARM, TIME).astype(jnp.bfloat16)


def lookup(material, table):
    values = jnp.zeros(material.shape, jnp.float32)
    for material_id in range(NMAT):
        values = jnp.where(material == material_id, table[material_id], values)
    return values


def face_value(conduct, other):
    other = jnp.where(other > 0, other, conduct)
    return 2.0 * conduct * other / (conduct + other)


def face_values(conduct, padded):
    next_x = face_value(conduct, padded[2:, 1:-1, 1:-1])
    prev_x = face_value(conduct, padded[:-2, 1:-1, 1:-1])
    next_y = face_value(conduct, padded[1:-1, 2:, 1:-1])
    prev_y = face_value(conduct, padded[1:-1, :-2, 1:-1])
    next_z = face_value(conduct, padded[1:-1, 1:-1, 2:])
    prev_z = face_value(conduct, padded[1:-1, 1:-1, :-2])
    total = next_x + prev_x + next_y + prev_y + next_z + prev_z
    return ((next_x, prev_x, next_y, prev_y, next_z, prev_z), total)


def relax_sweep(padded, source, faces, real_den, imag_den):
    next_x, prev_x, next_y, prev_y, next_z, prev_z = faces
    nearby = next_x * padded[..., 2:, 1:-1, 1:-1] + prev_x * padded[..., :-2, 1:-1, 1:-1]
    nearby = nearby + next_y * padded[..., 1:-1, 2:, 1:-1] + prev_y * padded[..., 1:-1, :-2, 1:-1]
    nearby = nearby + next_z * padded[..., 1:-1, 1:-1, 2:] + prev_z * padded[..., 1:-1, 1:-1, :-2]
    numerator = source + nearby
    real_num = numerator[..., 0, :, :, :]
    imag_num = numerator[..., 1, :, :, :]
    modulus = real_den * real_den + imag_den * imag_den
    real_out = (real_num * real_den + imag_num * imag_den) / modulus
    imag_out = (imag_num * real_den - real_num * imag_den) / modulus
    return jnp.stack([real_out, imag_out], axis=-4)


def to_harmonics(payload):
    transform_rows = dft_table()
    gathered = lax.all_to_all(payload, "tm", split_axis=1, concat_axis=0, tiled=True)
    flattened = gathered.reshape(TIME, gathered.shape[1] * gathered.shape[2])
    harmonic = jnp.dot(transform_rows, flattened, preferred_element_type=jnp.float32)
    harmonic = harmonic.astype(jnp.bfloat16).reshape(2 * HARM, gathered.shape[1], gathered.shape[2])
    return lax.all_to_all(harmonic, "tm", split_axis=0, concat_axis=1, tiled=True)


def to_owners(payload, owner_map, stencil_column):
    owners = lax.axis_size("sx") * lax.axis_size("sy")
    capacity_slots = 2 * payload.shape[1] // owners
    owner_ids = owner_map[:, 0]
    onehot = (owner_ids[:, None] == jnp.arange(owners, dtype=jnp.int32)[None, :]).astype(jnp.int32)
    rank_all = jnp.cumsum(onehot, axis=0) - onehot
    rank_own = jnp.sum(rank_all * onehot, axis=1)
    slot_index = owner_ids * capacity_slots + rank_own
    buffer = jnp.zeros((payload.shape[0], owners * capacity_slots, payload.shape[2]), jnp.bfloat16)
    buffer = buffer.at[:, slot_index, :].set(payload)
    columns = (
        jnp.full((1, owners * capacity_slots), -1, jnp.int32).at[0, slot_index].set(stencil_column)
    )
    return (
        lax.all_to_all(buffer, ("sx", "sy"), split_axis=1, concat_axis=1, tiled=True),
        lax.all_to_all(columns, ("sx", "sy"), split_axis=1, concat_axis=1, tiled=True),
    )


def body(wall_temp, owner_map, stencil_column, material, conductivity, capacity):
    received, columns = to_owners(wall_temp, owner_map, stencil_column)
    harmonic = to_harmonics(received)
    size_x, size_y, size_z = material.shape
    local_harms = harmonic.shape[0] // 2
    column_hits = (jnp.arange(size_x * size_y, dtype=jnp.int32)[:, None] == columns).astype(
        jnp.bfloat16
    )
    source = jnp.einsum("ps,csz->cpz", column_hits, harmonic, preferred_element_type=jnp.float32)
    source = source.reshape(local_harms, 2, size_x, size_y, size_z)
    conduct = lookup(material, conductivity)
    heat_cap = lookup(material, capacity)
    rim = with_halo(conduct.astype(jnp.bfloat16), (("sx", 0), ("sy", 1)), 1).astype(conduct.dtype)
    rim = jnp.pad(rim, ((0, 0), (0, 0), (1, 1)), mode="edge")
    faces, real_den = face_values(conduct, rim)
    harm_index = lax.axis_index("tm") * local_harms + jnp.arange(local_harms, dtype=jnp.int32)
    imag_den = omega_step * harm_index.astype(jnp.float32)[:, None, None, None] * heat_cap
    start = jnp.zeros((local_harms, 2, size_x + 2, size_y + 2, size_z + 2), jnp.float32)
    field = relax_sweep(start, source, faces, real_den, imag_den)
    for sweep in range(SWEEPS - 1):
        padded = with_halo(field, (("sx", 2), ("sy", 3)), 1)
        padded = jnp.pad(padded, ((0, 0), (0, 0), (0, 0), (0, 0), (1, 1)))
        field = relax_sweep(padded, source, faces, real_den, imag_den)
    return field


RADIX = 4
GROUP = 2


def zero_refs(cond, refs):
    @pl.when(cond)
    def _():
        for ref in refs:
            ref[...] = jnp.zeros(ref.shape, ref.dtype)


def relax_kernel(
    counts, cond_ref, cap_ref, cos_ref, sin_ref, mat_ref, rows_ref, out_ref,
    conduct, heat, cy_send, cx_recv, cy_recv, coef, real_den, part_a, part_b, source,
    field_a, field_b, x_send, x_recv, y_send, y_recv,
    c_ssem, c_rsem, x_ssem, x_rsem, y_ssem, y_rsem,
):
    size_x, size_y, size_z = mat_ref.shape
    harms = source.shape[0]
    groups = harms // GROUP
    place = {axis: lax.axis_index(axis) for axis in ("sx", "sy")}
    has = {
        axis: (place[axis] > 0, place[axis] < counts[axis] - 1) for axis in ("sx", "sy")
    }
    beside = {axis: (place[axis] - 1, place[axis] + 1) for axis in ("sx", "sy")}
    sides = [(axis, side) for axis in ("sx", "sy") for side in (0, 1)]

    barrier = pltpu.get_barrier_semaphore()
    expected = jnp.int32(0)
    for axis, side in sides:
        expected = expected + has[axis][side].astype(jnp.int32)

        @pl.when(has[axis][side])
        def _(axis=axis, side=side):
            pl.semaphore_signal(
                barrier, inc=1, device_id={axis: beside[axis][side]},
                device_id_type=pl.DeviceIdType.MESH,
            )

    for axis, (c_buf, f_buf) in {"sx": (cx_recv, x_recv), "sy": (cy_recv, y_recv)}.items():
        for side in (0, 1):
            zero_refs(
                jnp.logical_not(has[axis][side]),
                [c_buf.at[side]] + [f_buf.at[s, side] for s in range(SWEEPS - 1)],
            )

    def cell_values(x, carry):
        mat = mat_ref[x]
        con = jnp.zeros(mat.shape, jnp.float32)
        cap = jnp.zeros(mat.shape, jnp.float32)
        for m in range(NMAT):
            con = jnp.where(mat == m, cond_ref[m], con)
            cap = jnp.where(mat == m, cap_ref[m], cap)
        conduct[x] = con
        heat[x] = cap
        cy_send[0, pl.ds(x, 1), :] = con[0:1]
        cy_send[1, pl.ds(x, 1), :] = con[size_y - 1 :]
        return carry

    lax.fori_loop(0, size_x, cell_values, 0)
    pl.semaphore_wait(barrier, expected)

    def c_copy(axis, side, toward):
        if axis == "sx":
            src, dst = conduct.at[(size_x - 1) * side], cx_recv.at[1 - side]
        else:
            src, dst = cy_send.at[side], cy_recv.at[1 - side]
        slot = 0 if axis == "sx" else 1
        return pltpu.make_async_remote_copy(
            src_ref=src, dst_ref=dst, send_sem=c_ssem.at[slot, side],
            recv_sem=c_rsem.at[slot, 1 - side],
            device_id={axis: beside[axis][toward]}, device_id_type=pl.DeviceIdType.MESH,
        )

    def f_copy(s, g, axis, side, toward):
        send, recv, ssem, rsem = (
            (x_send, x_recv, x_ssem, x_rsem) if axis == "sx" else (y_send, y_recv, y_ssem, y_rsem)
        )
        part = pl.ds(g * GROUP, GROUP)
        return pltpu.make_async_remote_copy(
            src_ref=send.at[s, side, part], dst_ref=recv.at[s, 1 - side, part],
            send_sem=ssem.at[s, g, side], recv_sem=rsem.at[s, g, 1 - side],
            device_id={axis: beside[axis][toward]}, device_id_type=pl.DeviceIdType.MESH,
        )

    def each(fn):
        for axis, side in sides:

            @pl.when(has[axis][side])
            def _(axis=axis, side=side):
                fn(axis, side)

    each(lambda axis, side: c_copy(axis, side, side).start())

    quarter = rows_ref.shape[0] // RADIX

    def transform(x, carry):
        cells = pl.ds(pl.multiple_of(x * size_y, size_y), size_y)
        real = [None] * harms
        imag = [None] * harms
        for b in range(quarter):
            t0, t1, t2, t3 = [
                rows_ref[a * quarter + b, cells, :].astype(jnp.float32) for a in range(RADIX)
            ]
            even, odd = t0 + t2, t1 + t3
            turn_r, turn_i = t0 - t2, t3 - t1
            folded = ((even + odd, None), (turn_r, turn_i), (even - odd, None), (turn_r, -turn_i))
            for j in range(harms):
                c, n = cos_ref[j * quarter + b], sin_ref[j * quarter + b]
                fr, fi = folded[j % RADIX]
                if fi is None:
                    re, im = c * fr, n * fr
                else:
                    re, im = c * fr - n * fi, c * fi + n * fr
                real[j] = re if b == 0 else real[j] + re
                imag[j] = im if b == 0 else imag[j] + im
        for j in range(harms):
            source[j, 0, x] = real[j]
            source[j, 1, x] = imag[j]
        return carry

    lax.fori_loop(0, size_x, transform, 0)

    each(lambda axis, side: c_copy(axis, 1 - side, side).wait_recv())

    first = (lax.axis_index("tm") * harms).astype(jnp.float32)
    row = lax.broadcasted_iota(jnp.int32, (size_y, size_z), 0)
    lane = lax.broadcasted_iota(jnp.int32, (size_y, size_z), 1)

    def shift_y(value, low, high):
        up = jnp.where(row == size_y - 1, high, pltpu.roll(value, size_y - 1, 0))
        down = jnp.where(row == 0, low, pltpu.roll(value, 1, 0))
        return up, down

    def keep(s, h, x, real, imag, dst, pad):
        for r, value in enumerate((real, imag)):
            dst[h, r, x + pad] = value
            if s < SWEEPS - 1:
                y_send[s, 0, h, r, pl.ds(x, 1), :] = value[0:1]
                y_send[s, 1, h, r, pl.ds(x, 1), :] = value[size_y - 1 :]

    def prepare(x, carry):
        own = conduct[x]
        above = jnp.where(x == size_x - 1, cx_recv[1], conduct[jnp.minimum(x + 1, size_x - 1)])
        below = jnp.where(x == 0, cx_recv[0], conduct[jnp.maximum(x - 1, 0)])
        up, down = shift_y(own, cy_recv[0, pl.ds(x, 1), :], cy_recv[1, pl.ds(x, 1), :])
        right = jnp.where(lane == size_z - 1, own, pltpu.roll(own, size_z - 1, 1))
        left = jnp.where(lane == 0, own, pltpu.roll(own, 1, 1))
        total = None
        for i, other in enumerate((above, below, up, down, right, left)):
            face = face_value(own, other)
            total = face if total is None else total + face
            if i == 4:
                face = jnp.where(lane == size_z - 1, 0.0, face)
            if i == 5:
                face = jnp.where(lane == 0, 0.0, face)
            coef[i, x] = face
        cap = heat[x]
        for h in range(harms):
            imag_den = (omega_step * (first + h)) * cap
            inverse = 1.0 / (total * total + imag_den * imag_den)
            a, b = total * inverse, imag_den * inverse
            part_a[h, x] = a
            part_b[h, x] = b
            sr, si = source[h, 0, x], source[h, 1, x]
            keep(0, h, x, sr * a + si * b, si * a - sr * b, field_a, 1)
        return carry

    lax.fori_loop(0, size_x, prepare, 0)

    def send_group(s, g, field):
        for j in range(GROUP):
            h = g * GROUP + j
            for r in range(2):
                x_send[s, 0, h, r] = field[h, r, 1].astype(x_send.dtype)
                x_send[s, 1, h, r] = field[h, r, size_x].astype(x_send.dtype)
        each(lambda axis, side: f_copy(s, g, axis, side, side).start())

    def launch(g, carry):
        send_group(0, g, field_a)
        return carry

    lax.fori_loop(0, groups, launch, 0)

    for s in range(1, SWEEPS):
        old = field_a if s % 2 == 1 else field_b
        last = s == SWEEPS - 1
        new = out_ref if last else (field_b if s % 2 == 1 else field_a)
        pad = 0 if last else 1

        def sweep(g, carry, s=s, old=old, new=new, pad=pad, last=last):
            each(lambda axis, side: f_copy(s - 1, g, axis, 1 - side, side).wait_recv())
            for j in range(GROUP):
                h = g * GROUP + j
                for r in range(2):
                    old[h, r, 0] = x_recv[s - 1, 0, h, r].astype(jnp.float32)
                    old[h, r, size_x + 1] = x_recv[s - 1, 1, h, r].astype(jnp.float32)

            def plane(x, inner):
                faces = [coef[i, x] for i in range(6)]
                for j in range(GROUP):
                    h = g * GROUP + j
                    nums = []
                    for r in range(2):
                        own = old[h, r, x + 1]
                        up, down = shift_y(
                            own,
                            y_recv[s - 1, 0, h, r, pl.ds(x, 1), :],
                            y_recv[s - 1, 1, h, r, pl.ds(x, 1), :],
                        )
                        num = source[h, r, x] + faces[0] * old[h, r, x + 2]
                        num = num + faces[1] * old[h, r, x]
                        num = num + (faces[2] * up + faces[3] * down)
                        num = num + faces[4] * pltpu.roll(own, size_z - 1, 1)
                        num = num + faces[5] * pltpu.roll(own, 1, 1)
                        nums.append(num)
                    a, b = part_a[h, x], part_b[h, x]
                    keep(
                        s, h, x, nums[0] * a + nums[1] * b, nums[1] * a - nums[0] * b, new, pad
                    )
                return inner

            lax.fori_loop(0, size_x, plane, 0)
            if not last:
                send_group(s, g, new)
            return carry

        lax.fori_loop(0, groups, sweep, 0)

    each(lambda axis, side: c_copy(axis, side, side).wait_send())

    def finish(g, carry):
        for s in range(SWEEPS - 1):
            each(lambda axis, side, s=s: f_copy(s, g, axis, side, side).wait_send())
        return carry

    lax.fori_loop(0, groups, finish, 0)


def relax(rows, material, conductivity, capacity):
    size_x, size_y, size_z = material.shape
    harms = HARM // lax.axis_size("tm")
    groups = harms // GROUP
    quarter = TIME // RADIX
    table = dft_table().astype(jnp.float32).reshape(HARM, 2, TIME)[:, :, :quarter]
    table = lax.dynamic_slice_in_dim(table, lax.axis_index("tm") * harms, harms, 0)
    f32, bf16 = jnp.float32, jnp.bfloat16
    tile = (size_x, size_y, size_z)
    padded = (harms, 2, size_x + 2, size_y, size_z)
    x_edge = (SWEEPS - 1, 2, harms, 2, size_y, size_z)
    y_edge = (SWEEPS - 1, 2, harms, 2, size_x, size_z)
    dma = pltpu.SemaphoreType.DMA
    counts = {axis: lax.axis_size(axis) for axis in ("sx", "sy")}
    smem = pl.BlockSpec(memory_space=pltpu.SMEM)
    vmem = pl.BlockSpec(memory_space=pltpu.VMEM)
    return pl.pallas_call(
        functools.partial(relax_kernel, counts),
        out_shape=jax.ShapeDtypeStruct((harms, 2) + tile, f32),
        in_specs=[smem] * 4 + [vmem] * 2,
        out_specs=vmem,
        scratch_shapes=[
            pltpu.VMEM(tile, f32),
            pltpu.VMEM(tile, f32),
            pltpu.VMEM((2, size_x, size_z), f32),
            pltpu.VMEM((2, size_y, size_z), f32),
            pltpu.VMEM((2, size_x, size_z), f32),
            pltpu.VMEM((6,) + tile, f32),
            pltpu.VMEM(tile, f32),
            pltpu.VMEM((harms,) + tile, f32),
            pltpu.VMEM((harms,) + tile, f32),
            pltpu.VMEM((harms, 2) + tile, f32),
            pltpu.VMEM(padded, f32),
            pltpu.VMEM(padded, f32),
            pltpu.VMEM(x_edge, bf16),
            pltpu.VMEM(x_edge, bf16),
            pltpu.VMEM(y_edge, f32),
            pltpu.VMEM(y_edge, f32),
            dma((2, 2)),
            dma((2, 2)),
            dma((SWEEPS - 1, groups, 2)),
            dma((SWEEPS - 1, groups, 2)),
            dma((SWEEPS - 1, groups, 2)),
            dma((SWEEPS - 1, groups, 2)),
        ],
        compiler_params=pltpu.CompilerParams(
            collective_id=1, has_side_effects=True, vmem_limit_bytes=48 * 1024 * 1024
        ),
    )(
        conductivity,
        capacity,
        table[:, 0].reshape(-1),
        table[:, 1].reshape(-1),
        material,
        rows,
    )


def fast_body(wall_temp, owner_map, stencil_column, material, conductivity, capacity):
    cells = material.shape[0] * material.shape[1]
    total = cells * lax.axis_size("sx") * lax.axis_size("sy")
    target = owner_map[:, 0] * cells + stencil_column
    hits = (jnp.arange(total, dtype=jnp.int32)[:, None] == target[None, :]).astype(jnp.bfloat16)
    summed = jnp.einsum("sp,tpz->tsz", hits, wall_temp, preferred_element_type=jnp.float32)
    summed = summed.astype(jnp.bfloat16)
    mine = lax.psum_scatter(summed, ("sx", "sy"), scatter_dimension=1, tiled=True)
    rows = lax.all_gather(mine, "tm", axis=0, tiled=True)
    return relax(rows, material, conductivity, capacity)


def solution(mesh):
    in_specs = (
        P("tm", ("sx", "sy"), None),
        P(("sx", "sy"), None),
        P(("sx", "sy")),
        P("sx", "sy", None),
        P(),
        P(),
    )
    out_specs = P("tm", None, "sx", "sy", None)
    direct = mesh.shape["tm"] == RADIX and mesh.shape["sx"] == 2 and mesh.shape["sy"] == 4
    step = fast_body if direct else body
    return jax.shard_map(step, mesh=mesh, in_specs=in_specs, out_specs=out_specs, check_vma=False)
```

```python
import functools
import math

import jax
import jax.numpy as jnp
from jax import lax
from jax.experimental import pallas as pl
from jax.experimental.pallas import tpu as pltpu
from jax.sharding import PartitionSpec as P

TIME = 64
HARM = 32
NMAT = 4
SWEEPS = 4


omega_step = 0.1


def with_halo(block, sides, width):
    for axis, dim in sides:
        count = lax.axis_size(axis)
        forward = [(i, i + 1) for i in range(count - 1)]
        backward = [(target, source) for source, target in forward]
        low = lax.ppermute(
            lax.slice_in_dim(block, block.shape[dim] - width, None, axis=dim), axis, forward
        )
        high = lax.ppermute(lax.slice_in_dim(block, 0, width, axis=dim), axis, backward)
        block = jnp.concatenate([low, block, high], axis=dim)
    return block


def dft_table():
    freq_index = jnp.arange(HARM, dtype=jnp.int32)
    time_index = jnp.arange(TIME, dtype=jnp.int32)
    phase_int = freq_index[:, None] * time_index[None, :] % TIME
    angles = phase_int.astype(jnp.float32) * jnp.float32(2.0 * math.pi / TIME)
    amplitude = jnp.float32(2.0 / math.sqrt(TIME))
    table_rows = jnp.stack([amplitude * jnp.cos(angles), -amplitude * jnp.sin(angles)], axis=1)
    return table_rows.reshape(2 * HARM, TIME).astype(jnp.bfloat16)


def lookup(material, table):
    values = jnp.zeros(material.shape, jnp.float32)
    for material_id in range(NMAT):
        values = jnp.where(material == material_id, table[material_id], values)
    return values


def face_value(conduct, other):
    other = jnp.where(other > 0, other, conduct)
    return 2.0 * conduct * other / (conduct + other)


def face_values(conduct, padded):
    next_x = face_value(conduct, padded[2:, 1:-1, 1:-1])
    prev_x = face_value(conduct, padded[:-2, 1:-1, 1:-1])
    next_y = face_value(conduct, padded[1:-1, 2:, 1:-1])
    prev_y = face_value(conduct, padded[1:-1, :-2, 1:-1])
    next_z = face_value(conduct, padded[1:-1, 1:-1, 2:])
    prev_z = face_value(conduct, padded[1:-1, 1:-1, :-2])
    total = next_x + prev_x + next_y + prev_y + next_z + prev_z
    return ((next_x, prev_x, next_y, prev_y, next_z, prev_z), total)


def relax_sweep(padded, source, faces, real_den, imag_den):
    next_x, prev_x, next_y, prev_y, next_z, prev_z = faces
    nearby = next_x * padded[..., 2:, 1:-1, 1:-1] + prev_x * padded[..., :-2, 1:-1, 1:-1]
    nearby = nearby + next_y * padded[..., 1:-1, 2:, 1:-1] + prev_y * padded[..., 1:-1, :-2, 1:-1]
    nearby = nearby + next_z * padded[..., 1:-1, 1:-1, 2:] + prev_z * padded[..., 1:-1, 1:-1, :-2]
    numerator = source + nearby
    real_num = numerator[..., 0, :, :, :]
    imag_num = numerator[..., 1, :, :, :]
    modulus = real_den * real_den + imag_den * imag_den
    real_out = (real_num * real_den + imag_num * imag_den) / modulus
    imag_out = (imag_num * real_den - real_num * imag_den) / modulus
    return jnp.stack([real_out, imag_out], axis=-4)


def to_harmonics(payload):
    transform_rows = dft_table()
    gathered = lax.all_to_all(payload, "tm", split_axis=1, concat_axis=0, tiled=True)
    flattened = gathered.reshape(TIME, gathered.shape[1] * gathered.shape[2])
    harmonic = jnp.dot(transform_rows, flattened, preferred_element_type=jnp.float32)
    harmonic = harmonic.astype(jnp.bfloat16).reshape(2 * HARM, gathered.shape[1], gathered.shape[2])
    return lax.all_to_all(harmonic, "tm", split_axis=0, concat_axis=1, tiled=True)


def to_owners(payload, owner_map, stencil_column):
    owners = lax.axis_size("sx") * lax.axis_size("sy")
    capacity_slots = 2 * payload.shape[1] // owners
    owner_ids = owner_map[:, 0]
    onehot = (owner_ids[:, None] == jnp.arange(owners, dtype=jnp.int32)[None, :]).astype(jnp.int32)
    rank_all = jnp.cumsum(onehot, axis=0) - onehot
    rank_own = jnp.sum(rank_all * onehot, axis=1)
    slot_index = owner_ids * capacity_slots + rank_own
    buffer = jnp.zeros((payload.shape[0], owners * capacity_slots, payload.shape[2]), jnp.bfloat16)
    buffer = buffer.at[:, slot_index, :].set(payload)
    columns = (
        jnp.full((1, owners * capacity_slots), -1, jnp.int32).at[0, slot_index].set(stencil_column)
    )
    return (
        lax.all_to_all(buffer, ("sx", "sy"), split_axis=1, concat_axis=1, tiled=True),
        lax.all_to_all(columns, ("sx", "sy"), split_axis=1, concat_axis=1, tiled=True),
    )


def body(wall_temp, owner_map, stencil_column, material, conductivity, capacity):
    received, columns = to_owners(wall_temp, owner_map, stencil_column)
    harmonic = to_harmonics(received)
    size_x, size_y, size_z = material.shape
    local_harms = harmonic.shape[0] // 2
    column_hits = (jnp.arange(size_x * size_y, dtype=jnp.int32)[:, None] == columns).astype(
        jnp.bfloat16
    )
    source = jnp.einsum("ps,csz->cpz", column_hits, harmonic, preferred_element_type=jnp.float32)
    source = source.reshape(local_harms, 2, size_x, size_y, size_z)
    conduct = lookup(material, conductivity)
    heat_cap = lookup(material, capacity)
    rim = with_halo(conduct.astype(jnp.bfloat16), (("sx", 0), ("sy", 1)), 1).astype(conduct.dtype)
    rim = jnp.pad(rim, ((0, 0), (0, 0), (1, 1)), mode="edge")
    faces, real_den = face_values(conduct, rim)
    harm_index = lax.axis_index("tm") * local_harms + jnp.arange(local_harms, dtype=jnp.int32)
    imag_den = omega_step * harm_index.astype(jnp.float32)[:, None, None, None] * heat_cap
    start = jnp.zeros((local_harms, 2, size_x + 2, size_y + 2, size_z + 2), jnp.float32)
    field = relax_sweep(start, source, faces, real_den, imag_den)
    for sweep in range(SWEEPS - 1):
        padded = with_halo(field, (("sx", 2), ("sy", 3)), 1)
        padded = jnp.pad(padded, ((0, 0), (0, 0), (0, 0), (0, 0), (1, 1)))
        field = relax_sweep(padded, source, faces, real_den, imag_den)
    return field


RADIX = 4
GROUP = 2


def zero_refs(cond, refs):
    @pl.when(cond)
    def _():
        for ref in refs:
            ref[...] = jnp.zeros(ref.shape, ref.dtype)


def relax_kernel(
    counts, cond_ref, cap_ref, cos_ref, sin_ref, mat_ref, rows_ref, out_ref,
    conduct, heat, cy_send, cx_recv, cy_recv, coef, real_den, part_a, part_b, source,
    field_a, field_b, x_send, x_recv, y_send, y_recv,
    c_ssem, c_rsem, x_ssem, x_rsem, y_ssem, y_rsem,
):
    size_x, size_y, size_z = mat_ref.shape
    harms = source.shape[0]
    groups = harms // GROUP
    place = {axis: lax.axis_index(axis) for axis in ("sx", "sy")}
    has = {
        axis: (place[axis] > 0, place[axis] < counts[axis] - 1) for axis in ("sx", "sy")
    }
    beside = {axis: (place[axis] - 1, place[axis] + 1) for axis in ("sx", "sy")}
    sides = [(axis, side) for axis in ("sx", "sy") for side in (0, 1)]

    barrier = pltpu.get_barrier_semaphore()
    expected = jnp.int32(0)
    for axis, side in sides:
        expected = expected + has[axis][side].astype(jnp.int32)

        @pl.when(has[axis][side])
        def _(axis=axis, side=side):
            pl.semaphore_signal(
                barrier, inc=1, device_id={axis: beside[axis][side]},
                device_id_type=pl.DeviceIdType.MESH,
            )

    for axis, (c_buf, f_buf) in {"sx": (cx_recv, x_recv), "sy": (cy_recv, y_recv)}.items():
        for side in (0, 1):
            zero_refs(
                jnp.logical_not(has[axis][side]),
                [c_buf.at[side]] + [f_buf.at[s, side] for s in range(SWEEPS - 1)],
            )

    def cell_values(x, carry):
        mat = mat_ref[x]
        con = jnp.zeros(mat.shape, jnp.float32)
        cap = jnp.zeros(mat.shape, jnp.float32)
        for m in range(NMAT):
            con = jnp.where(mat == m, cond_ref[m], con)
            cap = jnp.where(mat == m, cap_ref[m], cap)
        conduct[x] = con
        heat[x] = cap
        cy_send[0, pl.ds(x, 1), :] = con[0:1]
        cy_send[1, pl.ds(x, 1), :] = con[size_y - 1 :]
        return carry

    lax.fori_loop(0, size_x, cell_values, 0)
    pl.semaphore_wait(barrier, expected)

    def c_copy(axis, side, toward):
        if axis == "sx":
            src, dst = conduct.at[(size_x - 1) * side], cx_recv.at[1 - side]
        else:
            src, dst = cy_send.at[side], cy_recv.at[1 - side]
        slot = 0 if axis == "sx" else 1
        return pltpu.make_async_remote_copy(
            src_ref=src, dst_ref=dst, send_sem=c_ssem.at[slot, side],
            recv_sem=c_rsem.at[slot, 1 - side],
            device_id={axis: beside[axis][toward]}, device_id_type=pl.DeviceIdType.MESH,
        )

    def f_copy(s, g, axis, side, toward):
        send, recv, ssem, rsem = (
            (x_send, x_recv, x_ssem, x_rsem) if axis == "sx" else (y_send, y_recv, y_ssem, y_rsem)
        )
        part = pl.ds(g * GROUP, GROUP)
        return pltpu.make_async_remote_copy(
            src_ref=send.at[s, side, part], dst_ref=recv.at[s, 1 - side, part],
            send_sem=ssem.at[s, g, side], recv_sem=rsem.at[s, g, 1 - side],
            device_id={axis: beside[axis][toward]}, device_id_type=pl.DeviceIdType.MESH,
        )

    def each(fn):
        for axis, side in sides:

            @pl.when(has[axis][side])
            def _(axis=axis, side=side):
                fn(axis, side)

    each(lambda axis, side: c_copy(axis, side, side).start())

    quarter = rows_ref.shape[0] // RADIX

    def transform(x, carry):
        cells = pl.ds(pl.multiple_of(x * size_y, size_y), size_y)
        real = [None] * harms
        imag = [None] * harms
        for b in range(quarter):
            t0, t1, t2, t3 = [
                rows_ref[a * quarter + b, cells, :].astype(jnp.float32) for a in range(RADIX)
            ]
            even, odd = t0 + t2, t1 + t3
            turn_r, turn_i = t0 - t2, t3 - t1
            folded = ((even + odd, None), (turn_r, turn_i), (even - odd, None), (turn_r, -turn_i))
            for j in range(harms):
                c, n = cos_ref[j * quarter + b], sin_ref[j * quarter + b]
                fr, fi = folded[j % RADIX]
                if fi is None:
                    re, im = c * fr, n * fr
                else:
                    re, im = c * fr - n * fi, c * fi + n * fr
                real[j] = re if b == 0 else real[j] + re
                imag[j] = im if b == 0 else imag[j] + im
        for j in range(harms):
            source[j, 0, x] = real[j]
            source[j, 1, x] = imag[j]
        return carry

    lax.fori_loop(0, size_x, transform, 0)

    each(lambda axis, side: c_copy(axis, 1 - side, side).wait_recv())

    first = (lax.axis_index("tm") * harms).astype(jnp.float32)
    row = lax.broadcasted_iota(jnp.int32, (size_y, size_z), 0)
    lane = lax.broadcasted_iota(jnp.int32, (size_y, size_z), 1)

    def shift_y(value, low, high):
        up = jnp.where(row == size_y - 1, high, pltpu.roll(value, size_y - 1, 0))
        down = jnp.where(row == 0, low, pltpu.roll(value, 1, 0))
        return up, down

    def keep(s, h, x, real, imag, dst, pad):
        for r, value in enumerate((real, imag)):
            dst[h, r, x + pad] = value
            if s < SWEEPS - 1:
                y_send[s, 0, h, r, pl.ds(x, 1), :] = value[0:1]
                y_send[s, 1, h, r, pl.ds(x, 1), :] = value[size_y - 1 :]

    def prepare(x, carry):
        own = conduct[x]
        above = jnp.where(x == size_x - 1, cx_recv[1], conduct[jnp.minimum(x + 1, size_x - 1)])
        below = jnp.where(x == 0, cx_recv[0], conduct[jnp.maximum(x - 1, 0)])
        up, down = shift_y(own, cy_recv[0, pl.ds(x, 1), :], cy_recv[1, pl.ds(x, 1), :])
        right = jnp.where(lane == size_z - 1, own, pltpu.roll(own, size_z - 1, 1))
        left = jnp.where(lane == 0, own, pltpu.roll(own, 1, 1))
        total = None
        for i, other in enumerate((above, below, up, down, right, left)):
            face = face_value(own, other)
            total = face if total is None else total + face
            if i == 4:
                face = jnp.where(lane == size_z - 1, 0.0, face)
            if i == 5:
                face = jnp.where(lane == 0, 0.0, face)
            coef[i, x] = face
        cap = heat[x]
        for h in range(harms):
            imag_den = (omega_step * (first + h)) * cap
            inverse = 1.0 / (total * total + imag_den * imag_den)
            a, b = total * inverse, imag_den * inverse
            part_a[h, x] = a
            part_b[h, x] = b
            sr, si = source[h, 0, x], source[h, 1, x]
            keep(0, h, x, sr * a + si * b, si * a - sr * b, field_a, 1)
        return carry

    lax.fori_loop(0, size_x, prepare, 0)

    def send_group(s, g, field):
        for j in range(GROUP):
            h = g * GROUP + j
            for r in range(2):
                x_send[s, 0, h, r] = field[h, r, 1].astype(x_send.dtype)
                x_send[s, 1, h, r] = field[h, r, size_x].astype(x_send.dtype)
        each(lambda axis, side: f_copy(s, g, axis, side, side).start())

    def launch(g, carry):
        send_group(0, g, field_a)
        return carry

    lax.fori_loop(0, groups, launch, 0)

    for s in range(1, SWEEPS):
        old = field_a if s % 2 == 1 else field_b
        last = s == SWEEPS - 1
        new = out_ref if last else (field_b if s % 2 == 1 else field_a)
        pad = 0 if last else 1

        def sweep(g, carry, s=s, old=old, new=new, pad=pad, last=last):
            each(lambda axis, side: f_copy(s - 1, g, axis, 1 - side, side).wait_recv())
            for j in range(GROUP):
                h = g * GROUP + j
                for r in range(2):
                    old[h, r, 0] = x_recv[s - 1, 0, h, r].astype(jnp.float32)
                    old[h, r, size_x + 1] = x_recv[s - 1, 1, h, r].astype(jnp.float32)

            def plane(x, inner):
                faces = [coef[i, x] for i in range(6)]
                for j in range(GROUP):
                    h = g * GROUP + j
                    nums = []
                    for r in range(2):
                        own = old[h, r, x + 1]
                        up, down = shift_y(
                            own,
                            y_recv[s - 1, 0, h, r, pl.ds(x, 1), :],
                            y_recv[s - 1, 1, h, r, pl.ds(x, 1), :],
                        )
                        num = source[h, r, x] + faces[0] * old[h, r, x + 2]
                        num = num + faces[1] * old[h, r, x]
                        num = num + (faces[2] * up + faces[3] * down)
                        num = num + faces[4] * pltpu.roll(own, size_z - 1, 1)
                        num = num + faces[5] * pltpu.roll(own, 1, 1)
                        nums.append(num)
                    a, b = part_a[h, x], part_b[h, x]
                    keep(
                        s, h, x, nums[0] * a + nums[1] * b, nums[1] * a - nums[0] * b, new, pad
                    )
                return inner

            lax.fori_loop(0, size_x, plane, 0)
            if not last:
                send_group(s, g, new)
            return carry

        lax.fori_loop(0, groups, sweep, 0)

    each(lambda axis, side: c_copy(axis, side, side).wait_send())

    def finish(g, carry):
        for s in range(SWEEPS - 1):
            each(lambda axis, side, s=s: f_copy(s, g, axis, side, side).wait_send())
        return carry

    lax.fori_loop(0, groups, finish, 0)


def relax(rows, material, conductivity, capacity):
    size_x, size_y, size_z = material.shape
    harms = HARM // lax.axis_size("tm")
    groups = harms // GROUP
    quarter = TIME // RADIX
    table = dft_table().astype(jnp.float32).reshape(HARM, 2, TIME)[:, :, :quarter]
    table = lax.dynamic_slice_in_dim(table, lax.axis_index("tm") * harms, harms, 0)
    f32, bf16 = jnp.float32, jnp.bfloat16
    tile = (size_x, size_y, size_z)
    padded = (harms, 2, size_x + 2, size_y, size_z)
    x_edge = (SWEEPS - 1, 2, harms, 2, size_y, size_z)
    y_edge = (SWEEPS - 1, 2, harms, 2, size_x, size_z)
    dma = pltpu.SemaphoreType.DMA
    counts = {axis: lax.axis_size(axis) for axis in ("sx", "sy")}
    smem = pl.BlockSpec(memory_space=pltpu.SMEM)
    vmem = pl.BlockSpec(memory_space=pltpu.VMEM)
    return pl.pallas_call(
        functools.partial(relax_kernel, counts),
        out_shape=jax.ShapeDtypeStruct((harms, 2) + tile, f32),
        in_specs=[smem] * 4 + [vmem] * 2,
        out_specs=vmem,
        scratch_shapes=[
            pltpu.VMEM(tile, f32),
            pltpu.VMEM(tile, f32),
            pltpu.VMEM((2, size_x, size_z), f32),
            pltpu.VMEM((2, size_y, size_z), f32),
            pltpu.VMEM((2, size_x, size_z), f32),
            pltpu.VMEM((6,) + tile, f32),
            pltpu.VMEM(tile, f32),
            pltpu.VMEM((harms,) + tile, f32),
            pltpu.VMEM((harms,) + tile, f32),
            pltpu.VMEM((harms, 2) + tile, f32),
            pltpu.VMEM(padded, f32),
            pltpu.VMEM(padded, f32),
            pltpu.VMEM(x_edge, bf16),
            pltpu.VMEM(x_edge, bf16),
            pltpu.VMEM(y_edge, f32),
            pltpu.VMEM(y_edge, f32),
            dma((2, 2)),
            dma((2, 2)),
            dma((SWEEPS - 1, groups, 2)),
            dma((SWEEPS - 1, groups, 2)),
            dma((SWEEPS - 1, groups, 2)),
            dma((SWEEPS - 1, groups, 2)),
        ],
        compiler_params=pltpu.CompilerParams(
            collective_id=1, has_side_effects=True, vmem_limit_bytes=48 * 1024 * 1024
        ),
    )(
        conductivity,
        capacity,
        table[:, 0].reshape(-1),
        table[:, 1].reshape(-1),
        material,
        rows,
    )


LAGS = (0, 1, 3, 5, 7, 9, 11)


def gather_kernel(
    target_ref, wall_ref, rows_ref,
    hits, core_send, core_recv, one_keep, one_send, one_recv, two_keep, two_send, two_recv,
    core_ssem, core_rsem, one_ssem, one_rsem, two_ssem, two_rsem, z_ssem, z_rsem,
):
    steps, patches, _ = wall_ref.shape
    cells = rows_ref.shape[1]
    tm, sx, sy = (lax.axis_index(axis) for axis in ("tm", "sx", "sy"))
    x, core = sy // 2, sy % 2
    mesh_id = pl.DeviceIdType.MESH
    last = RADIX - 1

    barrier = pltpu.get_barrier_semaphore()
    for peer in ((tm, sx, 2 * x + 1 - core), (tm, sx, 2 * (1 - x) + core), (tm, 1 - sx, sy)):
        pl.semaphore_signal(barrier, inc=1, device_id=peer, device_id_type=mesh_id)

    @pl.when(tm > 0)
    def _():
        pl.semaphore_signal(barrier, inc=1, device_id=(tm - 1, sx, sy), device_id_type=mesh_id)

    @pl.when(tm < last)
    def _():
        pl.semaphore_signal(barrier, inc=1, device_id=(tm + 1, sx, sy), device_id_type=mesh_id)

    strip = 64

    def mark(i, carry):
        ids = lax.broadcasted_iota(jnp.int32, (strip, patches), 0) + i * strip
        match = jnp.where(ids == target_ref[...], 1.0, 0.0)
        hits[pl.ds(pl.multiple_of(i * strip, strip), strip), :] = match.astype(jnp.bfloat16)
        return carry

    lax.fori_loop(0, hits.shape[0] // strip, mark, 0)
    pl.semaphore_wait(barrier, 3 + (tm > 0).astype(jnp.int32) + (tm < last).astype(jnp.int32))

    def flip(bit, odd):
        return bit + odd - 2 * bit * odd

    def tile_sum(c, u, v, own_core):
        turn = c % 2
        cell_x = flip(x, u + turn * (v - u))
        cell_y = flip(sx, v + turn * (u - v))
        owner = cell_y * 4 + cell_x * 2 + own_core
        part = hits[pl.ds(pl.multiple_of(owner * cells, cells), cells), :]
        return jnp.dot(part, wall_ref[c], preferred_element_type=jnp.float32)

    def core_copy(c):
        return pltpu.make_async_remote_copy(
            src_ref=core_send.at[c], dst_ref=core_recv.at[c],
            send_sem=core_ssem.at[c], recv_sem=core_rsem.at[c],
            device_id=(tm, sx, 2 * x + 1 - core), device_id_type=mesh_id,
        )

    def plane_copy(c, send, recv, ssem, rsem, along_y):
        peer = (tm, flip(sx, along_y), 2 * flip(x, 1 - along_y) + core)
        return pltpu.make_async_remote_copy(
            src_ref=send.at[c], dst_ref=recv.at[c], send_sem=ssem.at[c], recv_sem=rsem.at[c],
            device_id=peer, device_id_type=mesh_id,
        )

    def one_copy(c):
        return plane_copy(c, one_send, one_recv, one_ssem, one_rsem, c % 2)

    def two_copy(c):
        return plane_copy(c, two_send, two_recv, two_ssem, two_rsem, 1 - c % 2)

    def z_copy(c, down, block, hop, peer):
        place = block * steps + c
        return pltpu.make_async_remote_copy(
            src_ref=rows_ref.at[place], dst_ref=rows_ref.at[place],
            send_sem=z_ssem.at[down, hop, c], recv_sem=z_rsem.at[down, hop, c],
            device_id=(peer, sx, sy), device_id_type=mesh_id,
        )

    def z_send(c, hop, act):
        @pl.when(jnp.logical_and(tm < last, tm - hop >= 0))
        def _():
            act(z_copy(c, 0, tm - hop, hop, tm + 1))

        @pl.when(jnp.logical_and(tm > 0, tm + hop <= last))
        def _():
            act(z_copy(c, 1, tm + hop, hop, tm - 1))

    def z_arrive(c, hop):
        @pl.when(tm - hop - 1 >= 0)
        def _():
            z_copy(c, 0, tm - hop - 1, hop, tm - 1).wait_recv()

        @pl.when(tm + hop + 1 <= last)
        def _():
            z_copy(c, 1, tm + hop + 1, hop, tm + 1).wait_recv()

    def start(copy):
        copy.start()

    def for_partner(c):
        for u in range(2):
            for v in range(2):
                core_send[c, 2 * u + v] = tile_sum(c, u, v, 1 - core).astype(jnp.bfloat16)
        core_copy(c).start()

    def first_turn(c):
        core_copy(c).wait_recv()
        for u in (1, 0):
            for v in range(2):
                both = tile_sum(c, u, v, core) + core_recv[c, 2 * u + v].astype(jnp.float32)
                if u == 1:
                    one_send[c, v] = both.astype(jnp.bfloat16)
                else:
                    one_keep[c, v] = both
            if u == 1:
                one_copy(c).start()

    def second_turn(c):
        one_copy(c).wait_recv()
        two_send[c] = (one_keep[c, 1] + one_recv[c, 1].astype(jnp.float32)).astype(jnp.bfloat16)
        two_copy(c).start()
        two_keep[c] = one_keep[c, 0] + one_recv[c, 0].astype(jnp.float32)

    def complete(c):
        two_copy(c).wait_recv()
        total = two_keep[c] + two_recv[c].astype(jnp.float32)
        rows_ref[tm * steps + c] = total.astype(jnp.bfloat16)
        z_send(c, 0, start)

    def hop_one(c):
        z_arrive(c, 0)
        z_send(c, 1, start)

    def hop_two(c):
        z_arrive(c, 1)
        z_send(c, 2, start)

    def hop_three(c):
        z_arrive(c, 2)

    stages = (for_partner, first_turn, second_turn, complete, hop_one, hop_two, hop_three)

    def tick(i, carry):
        for lag, stage in reversed(list(zip(LAGS, stages))):

            @pl.when(jnp.logical_and(i >= lag, i < steps + lag))
            def _(lag=lag, stage=stage):
                stage(i - lag)

        return carry

    lax.fori_loop(0, steps + LAGS[-1], tick, 0)

    def drain(c, carry):
        core_copy(c).wait_send()
        one_copy(c).wait_send()
        two_copy(c).wait_send()
        for hop in range(RADIX - 1):
            z_send(c, hop, lambda copy: copy.wait_send())
        return carry

    lax.fori_loop(0, steps, drain, 0)


def gather_rows(target, wall_temp, cells, total):
    steps, patches, width = wall_temp.shape
    f32, bf16 = jnp.float32, jnp.bfloat16
    tile = (cells, width)
    dma = pltpu.SemaphoreType.DMA
    vmem = pl.BlockSpec(memory_space=pltpu.VMEM)
    return pl.pallas_call(
        gather_kernel,
        out_shape=jax.ShapeDtypeStruct((RADIX * steps,) + tile, bf16),
        in_specs=[vmem] * 2,
        out_specs=vmem,
        scratch_shapes=[
            pltpu.VMEM((total, patches), bf16),
            pltpu.VMEM((steps, 4) + tile, bf16),
            pltpu.VMEM((steps, 4) + tile, bf16),
            pltpu.VMEM((steps, 2) + tile, f32),
            pltpu.VMEM((steps, 2) + tile, bf16),
            pltpu.VMEM((steps, 2) + tile, bf16),
            pltpu.VMEM((steps,) + tile, f32),
            pltpu.VMEM((steps,) + tile, bf16),
            pltpu.VMEM((steps,) + tile, bf16),
        ]
        + [dma((steps,))] * 6
        + [dma((2, RADIX - 1, steps))] * 2,
        compiler_params=pltpu.CompilerParams(
            collective_id=2, has_side_effects=True, vmem_limit_bytes=50 * 1024 * 1024
        ),
    )(target[None, :], wall_temp)


def fast_body(wall_temp, owner_map, stencil_column, material, conductivity, capacity):
    cells = material.shape[0] * material.shape[1]
    total = cells * lax.axis_size("sx") * lax.axis_size("sy")
    target = owner_map[:, 0] * cells + stencil_column
    rows = gather_rows(target, wall_temp, cells, total)
    return relax(rows, material, conductivity, capacity)


def solution(mesh):
    in_specs = (
        P("tm", ("sx", "sy"), None),
        P(("sx", "sy"), None),
        P(("sx", "sy")),
        P("sx", "sy", None),
        P(),
        P(),
    )
    out_specs = P("tm", None, "sx", "sy", None)
    direct = mesh.shape["tm"] == RADIX and mesh.shape["sx"] == 2 and mesh.shape["sy"] == 4
    step = fast_body if direct else body
    return jax.shard_map(step, mesh=mesh, in_specs=in_specs, out_specs=out_specs, check_vma=False)
```

```python
import functools
import math

import jax
import jax.numpy as jnp
from jax import lax
from jax.experimental import pallas as pl
from jax.experimental.pallas import tpu as pltpu
from jax.sharding import PartitionSpec as P

TIME = 64
HARM = 32
NMAT = 4
SWEEPS = 4


omega_step = 0.1


def with_halo(block, sides, width):
    for axis, dim in sides:
        count = lax.axis_size(axis)
        forward = [(i, i + 1) for i in range(count - 1)]
        backward = [(target, source) for source, target in forward]
        low = lax.ppermute(
            lax.slice_in_dim(block, block.shape[dim] - width, None, axis=dim), axis, forward
        )
        high = lax.ppermute(lax.slice_in_dim(block, 0, width, axis=dim), axis, backward)
        block = jnp.concatenate([low, block, high], axis=dim)
    return block


def dft_table():
    freq_index = jnp.arange(HARM, dtype=jnp.int32)
    time_index = jnp.arange(TIME, dtype=jnp.int32)
    phase_int = freq_index[:, None] * time_index[None, :] % TIME
    angles = phase_int.astype(jnp.float32) * jnp.float32(2.0 * math.pi / TIME)
    amplitude = jnp.float32(2.0 / math.sqrt(TIME))
    table_rows = jnp.stack([amplitude * jnp.cos(angles), -amplitude * jnp.sin(angles)], axis=1)
    return table_rows.reshape(2 * HARM, TIME).astype(jnp.bfloat16)


def lookup(material, table):
    values = jnp.zeros(material.shape, jnp.float32)
    for material_id in range(NMAT):
        values = jnp.where(material == material_id, table[material_id], values)
    return values


def face_value(conduct, other):
    other = jnp.where(other > 0, other, conduct)
    return 2.0 * conduct * other / (conduct + other)


def face_values(conduct, padded):
    next_x = face_value(conduct, padded[2:, 1:-1, 1:-1])
    prev_x = face_value(conduct, padded[:-2, 1:-1, 1:-1])
    next_y = face_value(conduct, padded[1:-1, 2:, 1:-1])
    prev_y = face_value(conduct, padded[1:-1, :-2, 1:-1])
    next_z = face_value(conduct, padded[1:-1, 1:-1, 2:])
    prev_z = face_value(conduct, padded[1:-1, 1:-1, :-2])
    total = next_x + prev_x + next_y + prev_y + next_z + prev_z
    return ((next_x, prev_x, next_y, prev_y, next_z, prev_z), total)


def relax_sweep(padded, source, faces, real_den, imag_den):
    next_x, prev_x, next_y, prev_y, next_z, prev_z = faces
    nearby = next_x * padded[..., 2:, 1:-1, 1:-1] + prev_x * padded[..., :-2, 1:-1, 1:-1]
    nearby = nearby + next_y * padded[..., 1:-1, 2:, 1:-1] + prev_y * padded[..., 1:-1, :-2, 1:-1]
    nearby = nearby + next_z * padded[..., 1:-1, 1:-1, 2:] + prev_z * padded[..., 1:-1, 1:-1, :-2]
    numerator = source + nearby
    real_num = numerator[..., 0, :, :, :]
    imag_num = numerator[..., 1, :, :, :]
    modulus = real_den * real_den + imag_den * imag_den
    real_out = (real_num * real_den + imag_num * imag_den) / modulus
    imag_out = (imag_num * real_den - real_num * imag_den) / modulus
    return jnp.stack([real_out, imag_out], axis=-4)


def to_harmonics(payload):
    transform_rows = dft_table()
    gathered = lax.all_to_all(payload, "tm", split_axis=1, concat_axis=0, tiled=True)
    flattened = gathered.reshape(TIME, gathered.shape[1] * gathered.shape[2])
    harmonic = jnp.dot(transform_rows, flattened, preferred_element_type=jnp.float32)
    harmonic = harmonic.astype(jnp.bfloat16).reshape(2 * HARM, gathered.shape[1], gathered.shape[2])
    return lax.all_to_all(harmonic, "tm", split_axis=0, concat_axis=1, tiled=True)


def to_owners(payload, owner_map, stencil_column):
    owners = lax.axis_size("sx") * lax.axis_size("sy")
    capacity_slots = 2 * payload.shape[1] // owners
    owner_ids = owner_map[:, 0]
    onehot = (owner_ids[:, None] == jnp.arange(owners, dtype=jnp.int32)[None, :]).astype(jnp.int32)
    rank_all = jnp.cumsum(onehot, axis=0) - onehot
    rank_own = jnp.sum(rank_all * onehot, axis=1)
    slot_index = owner_ids * capacity_slots + rank_own
    buffer = jnp.zeros((payload.shape[0], owners * capacity_slots, payload.shape[2]), jnp.bfloat16)
    buffer = buffer.at[:, slot_index, :].set(payload)
    columns = (
        jnp.full((1, owners * capacity_slots), -1, jnp.int32).at[0, slot_index].set(stencil_column)
    )
    return (
        lax.all_to_all(buffer, ("sx", "sy"), split_axis=1, concat_axis=1, tiled=True),
        lax.all_to_all(columns, ("sx", "sy"), split_axis=1, concat_axis=1, tiled=True),
    )


def body(wall_temp, owner_map, stencil_column, material, conductivity, capacity):
    received, columns = to_owners(wall_temp, owner_map, stencil_column)
    harmonic = to_harmonics(received)
    size_x, size_y, size_z = material.shape
    local_harms = harmonic.shape[0] // 2
    column_hits = (jnp.arange(size_x * size_y, dtype=jnp.int32)[:, None] == columns).astype(
        jnp.bfloat16
    )
    source = jnp.einsum("ps,csz->cpz", column_hits, harmonic, preferred_element_type=jnp.float32)
    source = source.reshape(local_harms, 2, size_x, size_y, size_z)
    conduct = lookup(material, conductivity)
    heat_cap = lookup(material, capacity)
    rim = with_halo(conduct.astype(jnp.bfloat16), (("sx", 0), ("sy", 1)), 1).astype(conduct.dtype)
    rim = jnp.pad(rim, ((0, 0), (0, 0), (1, 1)), mode="edge")
    faces, real_den = face_values(conduct, rim)
    harm_index = lax.axis_index("tm") * local_harms + jnp.arange(local_harms, dtype=jnp.int32)
    imag_den = omega_step * harm_index.astype(jnp.float32)[:, None, None, None] * heat_cap
    start = jnp.zeros((local_harms, 2, size_x + 2, size_y + 2, size_z + 2), jnp.float32)
    field = relax_sweep(start, source, faces, real_den, imag_den)
    for sweep in range(SWEEPS - 1):
        padded = with_halo(field, (("sx", 2), ("sy", 3)), 1)
        padded = jnp.pad(padded, ((0, 0), (0, 0), (0, 0), (0, 0), (1, 1)))
        field = relax_sweep(padded, source, faces, real_den, imag_den)
    return field


RADIX = 4
GROUP = 2


def zero_refs(cond, refs):
    @pl.when(cond)
    def _():
        for ref in refs:
            ref[...] = jnp.zeros(ref.shape, ref.dtype)


LAGS = (1, 3, 5, 7, 9, 11)
FACES_AT = 3
RING = 4


def blade_kernel(
    counts, cond_ref, cap_ref, cos_ref, sin_ref, target_ref, wall_ref, mat_ref, out_ref,
    hits, core_own, core_send, core_recv, one_keep, one_send, one_recv,
    two_keep, two_send, two_recv, rows_ref,
    conduct, heat, cy_send, cx_recv, cy_recv, coef, part_a, part_b, source,
    field_a, field_b, x_send, x_recv, y_send, y_recv,
    core_ssem, core_rsem, one_ssem, one_rsem, two_ssem, two_rsem, z_ssem, z_rsem,
    c_ssem, c_rsem, x_ssem, x_rsem, y_ssem, y_rsem,
):
    steps, patches, _ = wall_ref.shape
    cells = rows_ref.shape[1]
    size_x, size_y, size_z = mat_ref.shape
    harms = source.shape[0]
    groups = harms // GROUP
    tm, sx, sy = (lax.axis_index(axis) for axis in ("tm", "sx", "sy"))
    x, core = sy // 2, sy % 2
    mesh_id = pl.DeviceIdType.MESH
    last = RADIX - 1
    place = {"sx": sx, "sy": sy}
    has = {axis: (place[axis] > 0, place[axis] < counts[axis] - 1) for axis in place}
    beside = {axis: (place[axis] - 1, place[axis] + 1) for axis in place}
    sides = [(axis, side) for axis in ("sx", "sy") for side in (0, 1)]
    inner = jnp.logical_and(has["sy"][0], has["sy"][1])

    barrier = pltpu.get_barrier_semaphore()

    def greet(*peer):
        pl.semaphore_signal(barrier, inc=1, device_id=peer, device_id_type=mesh_id)

    greet(tm, sx, 2 * x + 1 - core)
    greet(tm, sx, 2 * (1 - x) + core)
    greet(tm, 1 - sx, sy)
    pl.when(tm > 0)(lambda: greet(tm - 1, sx, sy))
    pl.when(tm < last)(lambda: greet(tm + 1, sx, sy))
    pl.when(inner)(lambda: greet(tm, sx, 3 - sy))
    expected = 3 + sum(flag.astype(jnp.int32) for flag in (tm > 0, tm < last, inner))

    for axis, (c_buf, f_buf) in {"sx": (cx_recv, x_recv), "sy": (cy_recv, y_recv)}.items():
        for side in (0, 1):
            zero_refs(
                jnp.logical_not(has[axis][side]),
                [c_buf.at[side]] + [f_buf.at[s, side] for s in range(SWEEPS - 1)],
            )

    strip = 64

    def mark(i, carry):
        ids = lax.broadcasted_iota(jnp.int32, (strip, patches), 0) + i * strip
        match = jnp.where(ids == target_ref[...], 1.0, 0.0)
        hits[pl.ds(pl.multiple_of(i * strip, strip), strip), :] = match.astype(jnp.bfloat16)
        return carry

    lax.fori_loop(0, hits.shape[0] // strip, mark, 0)

    def cell_values(x, carry):
        mat = mat_ref[x]
        con = jnp.zeros(mat.shape, jnp.float32)
        cap = jnp.zeros(mat.shape, jnp.float32)
        for m in range(NMAT):
            con = jnp.where(mat == m, cond_ref[m], con)
            cap = jnp.where(mat == m, cap_ref[m], cap)
        conduct[x] = con
        heat[x] = cap
        cy_send[0, pl.ds(x, 1), :] = con[0:1]
        cy_send[1, pl.ds(x, 1), :] = con[size_y - 1 :]
        return carry

    lax.fori_loop(0, size_x, cell_values, 0)

    def clear(h, carry):
        for r in range(2):
            source[h, r] = jnp.zeros((size_x, size_y, size_z), jnp.float32)
        return carry

    lax.fori_loop(0, harms, clear, 0)
    pl.semaphore_wait(barrier, expected)

    def flip(bit, odd):
        return bit + odd - 2 * bit * odd

    def pick(c, u, v):
        turn = c % 2
        cell_x = flip(x, u + turn * (v - u))
        cell_y = flip(sx, v + turn * (u - v))
        return cell_y * 2 + cell_x

    def core_copy(c):
        return pltpu.make_async_remote_copy(
            src_ref=core_send.at[c], dst_ref=core_recv.at[c],
            send_sem=core_ssem.at[c], recv_sem=core_rsem.at[c],
            device_id=(tm, sx, 2 * x + 1 - core), device_id_type=mesh_id,
        )

    def plane_copy(c, send, recv, ssem, rsem, along_y):
        peer = (tm, flip(sx, along_y), 2 * flip(x, 1 - along_y) + core)
        return pltpu.make_async_remote_copy(
            src_ref=send.at[c], dst_ref=recv.at[c], send_sem=ssem.at[c], recv_sem=rsem.at[c],
            device_id=peer, device_id_type=mesh_id,
        )

    def one_copy(c):
        return plane_copy(c, one_send, one_recv, one_ssem, one_rsem, c % 2)

    def two_copy(c):
        return plane_copy(c, two_send, two_recv, two_ssem, two_rsem, 1 - c % 2)

    def z_copy(c, down, block, hop, peer):
        place = block * steps + c
        return pltpu.make_async_remote_copy(
            src_ref=rows_ref.at[place], dst_ref=rows_ref.at[place],
            send_sem=z_ssem.at[down, hop, c], recv_sem=z_rsem.at[down, hop, c],
            device_id=(peer, sx, sy), device_id_type=mesh_id,
        )

    def z_send(c, hop, act):
        @pl.when(jnp.logical_and(tm < last, tm - hop >= 0))
        def _():
            act(z_copy(c, 0, tm - hop, hop, tm + 1))

        @pl.when(jnp.logical_and(tm > 0, tm + hop <= last))
        def _():
            act(z_copy(c, 1, tm + hop, hop, tm - 1))

    def z_arrive(c, hop):
        @pl.when(tm - hop - 1 >= 0)
        def _():
            z_copy(c, 0, tm - hop - 1, hop, tm - 1).wait_recv()

        @pl.when(tm + hop + 1 <= last)
        def _():
            z_copy(c, 1, tm + hop + 1, hop, tm + 1).wait_recv()

    def start(copy):
        copy.start()

    def c_copy(axis, side, toward):
        if axis == "sx":
            src, dst = conduct.at[(size_x - 1) * side], cx_recv.at[1 - side]
        else:
            src, dst = cy_send.at[side], cy_recv.at[1 - side]
        slot = 0 if axis == "sx" else 1
        return pltpu.make_async_remote_copy(
            src_ref=src, dst_ref=dst, send_sem=c_ssem.at[slot, side],
            recv_sem=c_rsem.at[slot, 1 - side],
            device_id={axis: beside[axis][toward]}, device_id_type=pl.DeviceIdType.MESH,
        )

    def f_copy(s, g, axis, side, toward):
        send, recv, ssem, rsem = (
            (x_send, x_recv, x_ssem, x_rsem) if axis == "sx" else (y_send, y_recv, y_ssem, y_rsem)
        )
        part = pl.ds(g * GROUP, GROUP)
        return pltpu.make_async_remote_copy(
            src_ref=send.at[s, side, part], dst_ref=recv.at[s, 1 - side, part],
            send_sem=ssem.at[s, g, side], recv_sem=rsem.at[s, g, 1 - side],
            device_id={axis: beside[axis][toward]}, device_id_type=pl.DeviceIdType.MESH,
        )

    def each(fn):
        for axis, side in sides:

            @pl.when(has[axis][side])
            def _(axis=axis, side=side):
                fn(axis, side)

    each(lambda axis, side: c_copy(axis, side, side).start())

    first = (lax.axis_index("tm") * harms).astype(jnp.float32)
    row = lax.broadcasted_iota(jnp.int32, (size_y, size_z), 0)
    lane = lax.broadcasted_iota(jnp.int32, (size_y, size_z), 1)

    def shift_y(value, low, high):
        up = jnp.where(row == size_y - 1, high, pltpu.roll(value, size_y - 1, 0))
        down = jnp.where(row == 0, low, pltpu.roll(value, 1, 0))
        return up, down

    def keep(s, h, x, real, imag, dst, pad):
        for r, value in enumerate((real, imag)):
            dst[h, r, x + pad] = value
            if s < SWEEPS - 1:
                y_send[s, 0, h, r, pl.ds(x, 1), :] = value[0:1]
                y_send[s, 1, h, r, pl.ds(x, 1), :] = value[size_y - 1 :]

    def set_faces(x, carry):
        own = conduct[x]
        above = jnp.where(x == size_x - 1, cx_recv[1], conduct[jnp.minimum(x + 1, size_x - 1)])
        below = jnp.where(x == 0, cx_recv[0], conduct[jnp.maximum(x - 1, 0)])
        up, down = shift_y(own, cy_recv[0, pl.ds(x, 1), :], cy_recv[1, pl.ds(x, 1), :])
        right = jnp.where(lane == size_z - 1, own, pltpu.roll(own, size_z - 1, 1))
        left = jnp.where(lane == 0, own, pltpu.roll(own, 1, 1))
        total = None
        for i, other in enumerate((above, below, up, down, right, left)):
            face = face_value(own, other)
            total = face if total is None else total + face
            if i == 4:
                face = jnp.where(lane == size_z - 1, 0.0, face)
            if i == 5:
                face = jnp.where(lane == 0, 0.0, face)
            coef[i, x] = face
        cap = heat[x]
        for h in range(harms):
            imag_den = (omega_step * (first + h)) * cap
            inverse = 1.0 / (total * total + imag_den * imag_den)
            a, b = total * inverse, imag_den * inverse
            part_a[h, x] = a
            part_b[h, x] = b
        return carry

    def for_partner(c):
        pair = jnp.concatenate([wall_ref[c], wall_ref[c + 1]], axis=1)

        def sums(own_core):
            rows = pl.ds(pl.multiple_of(own_core * (4 * cells), 4 * cells), 4 * cells)
            return jnp.dot(hits[rows, :], pair, preferred_element_type=jnp.float32)

        sent = sums(1 - core).astype(jnp.bfloat16)
        for n in range(2):
            core_send[c + n] = sent[:, n * size_z : (n + 1) * size_z].reshape(4, cells, size_z)
            core_copy(c + n).start()
        kept = sums(core)
        for n in range(2):
            core_own[(c + n) % RING] = kept[:, n * size_z : (n + 1) * size_z].reshape(
                4, cells, size_z
            )

    def first_turn(c):
        core_copy(c).wait_recv()
        for u in (1, 0):
            for v in range(2):
                tile = pick(c, u, v)
                both = core_own[c % RING, tile] + core_recv[c, tile].astype(jnp.float32)
                if u == 1:
                    one_send[c, v] = both.astype(jnp.bfloat16)
                else:
                    one_keep[c % RING, v] = both
            if u == 1:
                one_copy(c).start()

    def second_turn(c):
        one_copy(c).wait_recv()
        two_send[c] = (one_keep[c % RING, 1] + one_recv[c, 1].astype(jnp.float32)).astype(
            jnp.bfloat16
        )
        two_copy(c).start()
        two_keep[c % RING] = one_keep[c % RING, 0] + one_recv[c, 0].astype(jnp.float32)

    def complete(c):
        two_copy(c).wait_recv()
        total = two_keep[c % RING] + two_recv[c].astype(jnp.float32)
        rows_ref[tm * steps + c] = total.astype(jnp.bfloat16)
        z_send(c, 0, start)

    def hop_one(c):
        z_arrive(c, 0)
        z_send(c, 1, start)

    def hop_two(c):
        z_arrive(c, 1)
        z_send(c, 2, start)

    def transform(c):
        def plane(x, carry):
            span = pl.ds(pl.multiple_of(x * size_y, size_y), size_y)
            folded = []
            for b in (c - 1, c):
                t0, t1, t2, t3 = [
                    rows_ref[a * steps + b, span, :].astype(jnp.float32) for a in range(RADIX)
                ]
                even, odd = t0 + t2, t1 + t3
                turn_r, turn_i = t0 - t2, t3 - t1
                folded.append(
                    ((even + odd, None), (turn_r, turn_i), (even - odd, None), (turn_r, -turn_i))
                )
            for j in range(harms):
                real, imag = source[j, 0, x], source[j, 1, x]
                for n, b in enumerate((c - 1, c)):
                    co, si = cos_ref[j * steps + b], sin_ref[j * steps + b]
                    fr, fi = folded[n][j % RADIX]
                    real = real + co * fr
                    imag = imag + si * fr
                    if fi is not None:
                        real = real - si * fi
                        imag = imag + co * fi
                source[j, 0, x] = real
                source[j, 1, x] = imag
            return carry

        lax.fori_loop(0, size_x, plane, 0)

    def hop_three(c):
        z_arrive(c, 2)
        pl.when(c % 2 == 1)(lambda: transform(c))

    stages = (first_turn, second_turn, complete, hop_one, hop_two, hop_three)

    def at(i, lag, stage):
        live = jnp.logical_and(i >= lag, i < steps + lag)
        pl.when(live)(lambda: stage(i - lag))

    def tick(i, carry):
        for lag, stage in reversed(list(zip(LAGS[:-1], stages[:-1]))):
            at(i, lag, stage)
        pl.when(jnp.logical_and(i % 2 == 0, i < steps))(lambda: for_partner(i))

        @pl.when(i == FACES_AT)
        def _():
            each(lambda axis, side: c_copy(axis, 1 - side, side).wait_recv())
            lax.fori_loop(0, size_x, set_faces, 0)

        at(i, LAGS[-1], hop_three)
        return carry

    lax.fori_loop(0, steps + LAGS[-1], tick, 0)

    def prepare(x, carry):
        for h in range(harms):
            a, b = part_a[h, x], part_b[h, x]
            sr, si = source[h, 0, x], source[h, 1, x]
            keep(0, h, x, sr * a + si * b, si * a - sr * b, field_a, 1)
        return carry

    lax.fori_loop(0, size_x, prepare, 0)

    def send_group(s, g, field):
        for j in range(GROUP):
            h = g * GROUP + j
            for r in range(2):
                x_send[s, 0, h, r] = field[h, r, 1].astype(x_send.dtype)
                x_send[s, 1, h, r] = field[h, r, size_x].astype(x_send.dtype)
        each(lambda axis, side: f_copy(s, g, axis, side, side).start())

    def launch(g, carry):
        send_group(0, g, field_a)
        return carry

    lax.fori_loop(0, groups, launch, 0)

    for s in range(1, SWEEPS):
        old = field_a if s % 2 == 1 else field_b
        final = s == SWEEPS - 1
        new = out_ref if final else (field_b if s % 2 == 1 else field_a)
        pad = 0 if final else 1

        def sweep(g, carry, s=s, old=old, new=new, pad=pad, final=final):
            each(lambda axis, side: f_copy(s - 1, g, axis, 1 - side, side).wait_recv())
            for j in range(GROUP):
                h = g * GROUP + j
                for r in range(2):
                    old[h, r, 0] = x_recv[s - 1, 0, h, r].astype(jnp.float32)
                    old[h, r, size_x + 1] = x_recv[s - 1, 1, h, r].astype(jnp.float32)

            def plane(x, inner):
                faces = [coef[i, x] for i in range(6)]
                for j in range(GROUP):
                    h = g * GROUP + j
                    nums = []
                    for r in range(2):
                        own = old[h, r, x + 1]
                        up, down = shift_y(
                            own,
                            y_recv[s - 1, 0, h, r, pl.ds(x, 1), :],
                            y_recv[s - 1, 1, h, r, pl.ds(x, 1), :],
                        )
                        num = source[h, r, x] + faces[0] * old[h, r, x + 2]
                        num = num + faces[1] * old[h, r, x]
                        num = num + (faces[2] * up + faces[3] * down)
                        num = num + faces[4] * pltpu.roll(own, size_z - 1, 1)
                        num = num + faces[5] * pltpu.roll(own, 1, 1)
                        nums.append(num)
                    a, b = part_a[h, x], part_b[h, x]
                    keep(
                        s, h, x, nums[0] * a + nums[1] * b, nums[1] * a - nums[0] * b, new, pad
                    )
                return inner

            lax.fori_loop(0, size_x, plane, 0)
            if not final:
                send_group(s, g, new)
            return carry

        lax.fori_loop(0, groups, sweep, 0)

    each(lambda axis, side: c_copy(axis, side, side).wait_send())

    def finish(g, carry):
        for s in range(SWEEPS - 1):
            each(lambda axis, side, s=s: f_copy(s, g, axis, side, side).wait_send())
        return carry

    lax.fori_loop(0, groups, finish, 0)

    def drain(c, carry):
        core_copy(c).wait_send()
        one_copy(c).wait_send()
        two_copy(c).wait_send()
        for hop in range(RADIX - 1):
            z_send(c, hop, lambda copy: copy.wait_send())
        return carry

    lax.fori_loop(0, steps, drain, 0)


def fast_body(wall_temp, owner_map, stencil_column, material, conductivity, capacity):
    steps, patches, _ = wall_temp.shape
    size_x, size_y, size_z = material.shape
    cells = size_x * size_y
    total = cells * lax.axis_size("sx") * lax.axis_size("sy")
    owner = owner_map[:, 0]
    target = ((owner % 2) * (total // 2) + (owner // 2) * cells + stencil_column)[None, :]
    harms = HARM // lax.axis_size("tm")
    groups = harms // GROUP
    table = dft_table().astype(jnp.float32).reshape(HARM, 2, TIME)[:, :, :steps]
    table = lax.dynamic_slice_in_dim(table, lax.axis_index("tm") * harms, harms, 0)
    f32, bf16 = jnp.float32, jnp.bfloat16
    tile = (size_x, size_y, size_z)
    flat = (cells, size_z)
    padded = (harms, 2, size_x + 2, size_y, size_z)
    x_edge = (SWEEPS - 1, 2, harms, 2, size_y, size_z)
    y_edge = (SWEEPS - 1, 2, harms, 2, size_x, size_z)
    shapes = [
        ((total, patches), bf16),
        ((RING, 4) + flat, f32),
        ((steps, 4) + flat, bf16),
        ((steps, 4) + flat, bf16),
        ((RING, 2) + flat, f32),
        ((steps, 2) + flat, bf16),
        ((steps, 2) + flat, bf16),
        ((RING,) + flat, f32),
        ((steps,) + flat, bf16),
        ((steps,) + flat, bf16),
        ((RADIX * steps,) + flat, bf16),
        (tile, f32),
        (tile, f32),
        ((2, size_x, size_z), f32),
        ((2, size_y, size_z), f32),
        ((2, size_x, size_z), f32),
        ((6,) + tile, f32),
        ((harms,) + tile, f32),
        ((harms,) + tile, f32),
        ((harms, 2) + tile, f32),
        (padded, f32),
        (padded, f32),
        (x_edge, bf16),
        (x_edge, bf16),
        (y_edge, f32),
        (y_edge, f32),
    ]
    sems = (
        [(steps,)] * 6
        + [(2, RADIX - 1, steps)] * 2
        + [(2, 2)] * 2
        + [(SWEEPS - 1, groups, 2)] * 4
    )
    counts = {axis: lax.axis_size(axis) for axis in ("sx", "sy")}
    smem = pl.BlockSpec(memory_space=pltpu.SMEM)
    vmem = pl.BlockSpec(memory_space=pltpu.VMEM)
    return pl.pallas_call(
        functools.partial(blade_kernel, counts),
        out_shape=jax.ShapeDtypeStruct((harms, 2) + tile, f32),
        in_specs=[smem] * 4 + [vmem] * 3,
        out_specs=vmem,
        scratch_shapes=[pltpu.VMEM(*shape) for shape in shapes]
        + [pltpu.SemaphoreType.DMA(shape) for shape in sems],
        compiler_params=pltpu.CompilerParams(
            collective_id=1, has_side_effects=True, vmem_limit_bytes=58 * 1024 * 1024
        ),
    )(
        conductivity,
        capacity,
        table[:, 0].reshape(-1),
        table[:, 1].reshape(-1),
        target,
        wall_temp,
        material,
    )


def solution(mesh):
    in_specs = (
        P("tm", ("sx", "sy"), None),
        P(("sx", "sy"), None),
        P(("sx", "sy")),
        P("sx", "sy", None),
        P(),
        P(),
    )
    out_specs = P("tm", None, "sx", "sy", None)
    direct = mesh.shape["tm"] == RADIX and mesh.shape["sx"] == 2 and mesh.shape["sy"] == 4
    step = fast_body if direct else body
    return jax.shard_map(step, mesh=mesh, in_specs=in_specs, out_specs=out_specs, check_vma=False)
```

```python
import functools
import math

import jax
import jax.numpy as jnp
from jax import lax
from jax.experimental import pallas as pl
from jax.experimental.pallas import tpu as pltpu
from jax.sharding import PartitionSpec as P

TIME = 64
HARM = 32
NMAT = 4
SWEEPS = 4


omega_step = 0.1


def with_halo(block, sides, width):
    for axis, dim in sides:
        count = lax.axis_size(axis)
        forward = [(i, i + 1) for i in range(count - 1)]
        backward = [(target, source) for source, target in forward]
        low = lax.ppermute(
            lax.slice_in_dim(block, block.shape[dim] - width, None, axis=dim), axis, forward
        )
        high = lax.ppermute(lax.slice_in_dim(block, 0, width, axis=dim), axis, backward)
        block = jnp.concatenate([low, block, high], axis=dim)
    return block


def dft_table():
    freq_index = jnp.arange(HARM, dtype=jnp.int32)
    time_index = jnp.arange(TIME, dtype=jnp.int32)
    phase_int = freq_index[:, None] * time_index[None, :] % TIME
    angles = phase_int.astype(jnp.float32) * jnp.float32(2.0 * math.pi / TIME)
    amplitude = jnp.float32(2.0 / math.sqrt(TIME))
    table_rows = jnp.stack([amplitude * jnp.cos(angles), -amplitude * jnp.sin(angles)], axis=1)
    return table_rows.reshape(2 * HARM, TIME).astype(jnp.bfloat16)


def lookup(material, table):
    values = jnp.zeros(material.shape, jnp.float32)
    for material_id in range(NMAT):
        values = jnp.where(material == material_id, table[material_id], values)
    return values


def face_value(conduct, other):
    other = jnp.where(other > 0, other, conduct)
    return 2.0 * conduct * other / (conduct + other)


def face_values(conduct, padded):
    next_x = face_value(conduct, padded[2:, 1:-1, 1:-1])
    prev_x = face_value(conduct, padded[:-2, 1:-1, 1:-1])
    next_y = face_value(conduct, padded[1:-1, 2:, 1:-1])
    prev_y = face_value(conduct, padded[1:-1, :-2, 1:-1])
    next_z = face_value(conduct, padded[1:-1, 1:-1, 2:])
    prev_z = face_value(conduct, padded[1:-1, 1:-1, :-2])
    total = next_x + prev_x + next_y + prev_y + next_z + prev_z
    return ((next_x, prev_x, next_y, prev_y, next_z, prev_z), total)


def relax_sweep(padded, source, faces, real_den, imag_den):
    next_x, prev_x, next_y, prev_y, next_z, prev_z = faces
    nearby = next_x * padded[..., 2:, 1:-1, 1:-1] + prev_x * padded[..., :-2, 1:-1, 1:-1]
    nearby = nearby + next_y * padded[..., 1:-1, 2:, 1:-1] + prev_y * padded[..., 1:-1, :-2, 1:-1]
    nearby = nearby + next_z * padded[..., 1:-1, 1:-1, 2:] + prev_z * padded[..., 1:-1, 1:-1, :-2]
    numerator = source + nearby
    real_num = numerator[..., 0, :, :, :]
    imag_num = numerator[..., 1, :, :, :]
    modulus = real_den * real_den + imag_den * imag_den
    real_out = (real_num * real_den + imag_num * imag_den) / modulus
    imag_out = (imag_num * real_den - real_num * imag_den) / modulus
    return jnp.stack([real_out, imag_out], axis=-4)


def to_harmonics(payload):
    transform_rows = dft_table()
    gathered = lax.all_to_all(payload, "tm", split_axis=1, concat_axis=0, tiled=True)
    flattened = gathered.reshape(TIME, gathered.shape[1] * gathered.shape[2])
    harmonic = jnp.dot(transform_rows, flattened, preferred_element_type=jnp.float32)
    harmonic = harmonic.astype(jnp.bfloat16).reshape(2 * HARM, gathered.shape[1], gathered.shape[2])
    return lax.all_to_all(harmonic, "tm", split_axis=0, concat_axis=1, tiled=True)


def to_owners(payload, owner_map, stencil_column):
    owners = lax.axis_size("sx") * lax.axis_size("sy")
    capacity_slots = 2 * payload.shape[1] // owners
    owner_ids = owner_map[:, 0]
    onehot = (owner_ids[:, None] == jnp.arange(owners, dtype=jnp.int32)[None, :]).astype(jnp.int32)
    rank_all = jnp.cumsum(onehot, axis=0) - onehot
    rank_own = jnp.sum(rank_all * onehot, axis=1)
    slot_index = owner_ids * capacity_slots + rank_own
    buffer = jnp.zeros((payload.shape[0], owners * capacity_slots, payload.shape[2]), jnp.bfloat16)
    buffer = buffer.at[:, slot_index, :].set(payload)
    columns = (
        jnp.full((1, owners * capacity_slots), -1, jnp.int32).at[0, slot_index].set(stencil_column)
    )
    return (
        lax.all_to_all(buffer, ("sx", "sy"), split_axis=1, concat_axis=1, tiled=True),
        lax.all_to_all(columns, ("sx", "sy"), split_axis=1, concat_axis=1, tiled=True),
    )


def body(wall_temp, owner_map, stencil_column, material, conductivity, capacity):
    received, columns = to_owners(wall_temp, owner_map, stencil_column)
    harmonic = to_harmonics(received)
    size_x, size_y, size_z = material.shape
    local_harms = harmonic.shape[0] // 2
    column_hits = (jnp.arange(size_x * size_y, dtype=jnp.int32)[:, None] == columns).astype(
        jnp.bfloat16
    )
    source = jnp.einsum("ps,csz->cpz", column_hits, harmonic, preferred_element_type=jnp.float32)
    source = source.reshape(local_harms, 2, size_x, size_y, size_z)
    conduct = lookup(material, conductivity)
    heat_cap = lookup(material, capacity)
    rim = with_halo(conduct.astype(jnp.bfloat16), (("sx", 0), ("sy", 1)), 1).astype(conduct.dtype)
    rim = jnp.pad(rim, ((0, 0), (0, 0), (1, 1)), mode="edge")
    faces, real_den = face_values(conduct, rim)
    harm_index = lax.axis_index("tm") * local_harms + jnp.arange(local_harms, dtype=jnp.int32)
    imag_den = omega_step * harm_index.astype(jnp.float32)[:, None, None, None] * heat_cap
    start = jnp.zeros((local_harms, 2, size_x + 2, size_y + 2, size_z + 2), jnp.float32)
    field = relax_sweep(start, source, faces, real_den, imag_den)
    for sweep in range(SWEEPS - 1):
        padded = with_halo(field, (("sx", 2), ("sy", 3)), 1)
        padded = jnp.pad(padded, ((0, 0), (0, 0), (0, 0), (0, 0), (1, 1)))
        field = relax_sweep(padded, source, faces, real_den, imag_den)
    return field


RADIX = 4
GROUP = 2


def planes(count, body, width):
    def block(i, carry):
        for n in range(width):
            body(i * width + n, 0)
        return carry

    lax.fori_loop(0, count // width, block, 0)


def zero_refs(cond, refs):
    @pl.when(cond)
    def _():
        for ref in refs:
            ref[...] = jnp.zeros(ref.shape, ref.dtype)


LAGS = (2, 5, 8, 11, 14, 17)
FACES_AT = 4
RING = 4


def blade_kernel(
    counts, cond_ref, cap_ref, cos_ref, sin_ref, target_ref, wall_ref, mat_ref, out_ref,
    hits, core_own, core_send, core_recv, one_keep, one_send, one_recv,
    two_keep, two_send, two_recv, rows_ref,
    conduct, heat, cy_send, cx_recv, cy_recv, coef, part_a, part_b, source,
    field_a, field_b, x_send, x_recv, y_send, y_recv,
    core_ssem, core_rsem, one_ssem, one_rsem, two_ssem, two_rsem, z_ssem, z_rsem,
    c_ssem, c_rsem, x_ssem, x_rsem, y_ssem, y_rsem,
):
    steps, patches, _ = wall_ref.shape
    cells = rows_ref.shape[1]
    size_x, size_y, size_z = mat_ref.shape
    harms = source.shape[0]
    groups = harms // GROUP
    tm, sx, sy = (lax.axis_index(axis) for axis in ("tm", "sx", "sy"))
    x, core = sy // 2, sy % 2
    mesh_id = pl.DeviceIdType.MESH
    last = RADIX - 1
    place = {"sx": sx, "sy": sy}
    has = {axis: (place[axis] > 0, place[axis] < counts[axis] - 1) for axis in place}
    beside = {axis: (place[axis] - 1, place[axis] + 1) for axis in place}
    sides = [(axis, side) for axis in ("sx", "sy") for side in (0, 1)]
    inner = jnp.logical_and(has["sy"][0], has["sy"][1])

    barrier = pltpu.get_barrier_semaphore()

    def greet(*peer):
        pl.semaphore_signal(barrier, inc=1, device_id=peer, device_id_type=mesh_id)

    greet(tm, sx, 2 * x + 1 - core)
    greet(tm, sx, 2 * (1 - x) + core)
    greet(tm, 1 - sx, sy)
    pl.when(tm > 0)(lambda: greet(tm - 1, sx, sy))
    pl.when(tm < last)(lambda: greet(tm + 1, sx, sy))
    pl.when(inner)(lambda: greet(tm, sx, 3 - sy))
    expected = 3 + sum(flag.astype(jnp.int32) for flag in (tm > 0, tm < last, inner))

    for axis, (c_buf, f_buf) in {"sx": (cx_recv, x_recv), "sy": (cy_recv, y_recv)}.items():
        for side in (0, 1):
            zero_refs(
                jnp.logical_not(has[axis][side]),
                [c_buf.at[side]] + [f_buf.at[s, side] for s in range(SWEEPS - 1)],
            )

    strip = 64

    def mark(i, carry):
        ids = lax.broadcasted_iota(jnp.int32, (strip, patches), 0) + i * strip
        match = jnp.where(ids == target_ref[...], 1.0, 0.0)
        hits[pl.ds(pl.multiple_of(i * strip, strip), strip), :] = match.astype(jnp.bfloat16)
        return carry

    lax.fori_loop(0, hits.shape[0] // strip, mark, 0)

    def cell_values(x, carry):
        mat = mat_ref[x]
        con = jnp.zeros(mat.shape, jnp.float32)
        cap = jnp.zeros(mat.shape, jnp.float32)
        for m in range(NMAT):
            con = jnp.where(mat == m, cond_ref[m], con)
            cap = jnp.where(mat == m, cap_ref[m], cap)
        conduct[x] = con
        heat[x] = cap
        cy_send[0, pl.ds(x, 1), :] = con[0:1]
        cy_send[1, pl.ds(x, 1), :] = con[size_y - 1 :]
        return carry

    lax.fori_loop(0, size_x, cell_values, 0)

    def clear(h, carry):
        for r in range(2):
            source[h, r] = jnp.zeros((size_x, size_y, size_z), jnp.float32)
        return carry

    lax.fori_loop(0, harms, clear, 0)
    pl.semaphore_wait(barrier, expected)

    def flip(bit, odd):
        return bit + odd - 2 * bit * odd

    def pick(c, u, v):
        turn = c % 2
        cell_x = flip(x, u + turn * (v - u))
        cell_y = flip(sx, v + turn * (u - v))
        return cell_y * 2 + cell_x

    def core_copy(c):
        return pltpu.make_async_remote_copy(
            src_ref=core_send.at[c], dst_ref=core_recv.at[c],
            send_sem=core_ssem.at[c], recv_sem=core_rsem.at[c],
            device_id=(tm, sx, 2 * x + 1 - core), device_id_type=mesh_id,
        )

    def plane_copy(c, send, recv, ssem, rsem, along_y):
        peer = (tm, flip(sx, along_y), 2 * flip(x, 1 - along_y) + core)
        return pltpu.make_async_remote_copy(
            src_ref=send.at[c], dst_ref=recv.at[c], send_sem=ssem.at[c], recv_sem=rsem.at[c],
            device_id=peer, device_id_type=mesh_id,
        )

    def one_copy(c):
        return plane_copy(c, one_send, one_recv, one_ssem, one_rsem, c % 2)

    def two_copy(c):
        return plane_copy(c, two_send, two_recv, two_ssem, two_rsem, 1 - c % 2)

    def z_copy(c, down, block, hop, peer):
        place = block * steps + c
        return pltpu.make_async_remote_copy(
            src_ref=rows_ref.at[place], dst_ref=rows_ref.at[place],
            send_sem=z_ssem.at[down, hop, c], recv_sem=z_rsem.at[down, hop, c],
            device_id=(peer, sx, sy), device_id_type=mesh_id,
        )

    def z_send(c, hop, act):
        @pl.when(jnp.logical_and(tm < last, tm - hop >= 0))
        def _():
            act(z_copy(c, 0, tm - hop, hop, tm + 1))

        @pl.when(jnp.logical_and(tm > 0, tm + hop <= last))
        def _():
            act(z_copy(c, 1, tm + hop, hop, tm - 1))

    def z_arrive(c, hop):
        @pl.when(tm - hop - 1 >= 0)
        def _():
            z_copy(c, 0, tm - hop - 1, hop, tm - 1).wait_recv()

        @pl.when(tm + hop + 1 <= last)
        def _():
            z_copy(c, 1, tm + hop + 1, hop, tm + 1).wait_recv()

    def start(copy):
        copy.start()

    def c_copy(axis, side, toward):
        if axis == "sx":
            src, dst = conduct.at[(size_x - 1) * side], cx_recv.at[1 - side]
        else:
            src, dst = cy_send.at[side], cy_recv.at[1 - side]
        slot = 0 if axis == "sx" else 1
        return pltpu.make_async_remote_copy(
            src_ref=src, dst_ref=dst, send_sem=c_ssem.at[slot, side],
            recv_sem=c_rsem.at[slot, 1 - side],
            device_id={axis: beside[axis][toward]}, device_id_type=pl.DeviceIdType.MESH,
        )

    def f_copy(s, g, axis, side, toward):
        send, recv, ssem, rsem = (
            (x_send, x_recv, x_ssem, x_rsem) if axis == "sx" else (y_send, y_recv, y_ssem, y_rsem)
        )
        part = pl.ds(g * GROUP, GROUP)
        return pltpu.make_async_remote_copy(
            src_ref=send.at[s, side, part], dst_ref=recv.at[s, 1 - side, part],
            send_sem=ssem.at[s, g, side], recv_sem=rsem.at[s, g, 1 - side],
            device_id={axis: beside[axis][toward]}, device_id_type=pl.DeviceIdType.MESH,
        )

    def each(fn):
        for axis, side in sides:

            @pl.when(has[axis][side])
            def _(axis=axis, side=side):
                fn(axis, side)

    each(lambda axis, side: c_copy(axis, side, side).start())

    first = (lax.axis_index("tm") * harms).astype(jnp.float32)
    row = lax.broadcasted_iota(jnp.int32, (size_y, size_z), 0)
    lane = lax.broadcasted_iota(jnp.int32, (size_y, size_z), 1)

    def shift_y(value, low, high):
        up = jnp.where(row == size_y - 1, high, pltpu.roll(value, size_y - 1, 0))
        down = jnp.where(row == 0, low, pltpu.roll(value, 1, 0))
        return up, down

    def keep(s, h, x, real, imag, dst, pad):
        for r, value in enumerate((real, imag)):
            dst[h, r, x + pad] = value
            if s < SWEEPS - 1:
                y_send[s, 0, h, r, pl.ds(x, 1), :] = value[0:1]
                y_send[s, 1, h, r, pl.ds(x, 1), :] = value[size_y - 1 :]

    def set_faces(x, carry):
        own = conduct[x]
        above = jnp.where(x == size_x - 1, cx_recv[1], conduct[jnp.minimum(x + 1, size_x - 1)])
        below = jnp.where(x == 0, cx_recv[0], conduct[jnp.maximum(x - 1, 0)])
        up, down = shift_y(own, cy_recv[0, pl.ds(x, 1), :], cy_recv[1, pl.ds(x, 1), :])
        right = jnp.where(lane == size_z - 1, own, pltpu.roll(own, size_z - 1, 1))
        left = jnp.where(lane == 0, own, pltpu.roll(own, 1, 1))
        total = None
        for i, other in enumerate((above, below, up, down, right, left)):
            face = face_value(own, other)
            total = face if total is None else total + face
            if i == 4:
                face = jnp.where(lane == size_z - 1, 0.0, face)
            if i == 5:
                face = jnp.where(lane == 0, 0.0, face)
            coef[i, x] = face
        cap = heat[x]
        for h in range(harms):
            imag_den = (omega_step * (first + h)) * cap
            inverse = 1.0 / (total * total + imag_den * imag_den)
            a, b = total * inverse, imag_den * inverse
            part_a[h, x] = a
            part_b[h, x] = b
        return carry

    def for_partner(c):
        pair = jnp.concatenate([wall_ref[c], wall_ref[c + 1]], axis=1)

        def sums(own_core):
            rows = pl.ds(pl.multiple_of(own_core * (4 * cells), 4 * cells), 4 * cells)
            return jnp.dot(hits[rows, :], pair, preferred_element_type=jnp.float32)

        sent = sums(1 - core).astype(jnp.bfloat16)
        for n in range(2):
            core_send[c + n] = sent[:, n * size_z : (n + 1) * size_z].reshape(4, cells, size_z)
            core_copy(c + n).start()
        kept = sums(core)
        for n in range(2):
            core_own[(c + n) % RING] = kept[:, n * size_z : (n + 1) * size_z].reshape(
                4, cells, size_z
            )

    def first_turn(c):
        core_copy(c).wait_recv()
        for u in (1, 0):
            for v in range(2):
                tile = pick(c, u, v)
                both = core_own[c % RING, tile] + core_recv[c, tile].astype(jnp.float32)
                if u == 1:
                    one_send[c, v] = both.astype(jnp.bfloat16)
                else:
                    one_keep[c % RING, v] = both
            if u == 1:
                one_copy(c).start()

    def second_turn(c):
        one_copy(c).wait_recv()
        two_send[c] = (one_keep[c % RING, 1] + one_recv[c, 1].astype(jnp.float32)).astype(
            jnp.bfloat16
        )
        two_copy(c).start()
        two_keep[c % RING] = one_keep[c % RING, 0] + one_recv[c, 0].astype(jnp.float32)

    def complete(c):
        two_copy(c).wait_recv()
        total = two_keep[c % RING] + two_recv[c].astype(jnp.float32)
        rows_ref[tm * steps + c] = total.astype(jnp.bfloat16)
        z_send(c, 0, start)

    def hop_one(c):
        z_arrive(c, 0)
        z_send(c, 1, start)

    def hop_two(c):
        z_arrive(c, 1)
        z_send(c, 2, start)

    def transform(c):
        def plane(x, carry):
            span = pl.ds(pl.multiple_of(x * size_y, size_y), size_y)
            folded = []
            for b in (c - 1, c):
                t0, t1, t2, t3 = [
                    rows_ref[a * steps + b, span, :].astype(jnp.float32) for a in range(RADIX)
                ]
                even, odd = t0 + t2, t1 + t3
                turn_r, turn_i = t0 - t2, t3 - t1
                folded.append(
                    ((even + odd, None), (turn_r, turn_i), (even - odd, None), (turn_r, -turn_i))
                )
            for j in range(harms):
                real, imag = source[j, 0, x], source[j, 1, x]
                for n, b in enumerate((c - 1, c)):
                    co, si = cos_ref[j * steps + b], sin_ref[j * steps + b]
                    fr, fi = folded[n][j % RADIX]
                    real = real + co * fr
                    imag = imag + si * fr
                    if fi is not None:
                        real = real - si * fi
                        imag = imag + co * fi
                source[j, 0, x] = real
                source[j, 1, x] = imag
            return carry

        planes(size_x, plane, 2)

    def hop_three(c):
        z_arrive(c, 2)
        pl.when(c % 2 == 1)(lambda: transform(c))

    stages = (first_turn, second_turn, complete, hop_one, hop_two, hop_three)

    def at(i, lag, stage):
        live = jnp.logical_and(i >= lag, i < steps + lag)
        pl.when(live)(lambda: stage(i - lag))

    def tick(i, carry):
        for lag, stage in reversed(list(zip(LAGS[:-1], stages[:-1]))):
            at(i, lag, stage)
        pl.when(jnp.logical_and(i % 2 == 0, i < steps))(lambda: for_partner(i))

        @pl.when(i == FACES_AT)
        def _():
            each(lambda axis, side: c_copy(axis, 1 - side, side).wait_recv())
            planes(size_x, set_faces, 2)

        at(i, LAGS[-1], hop_three)
        return carry

    lax.fori_loop(0, steps + LAGS[-1], tick, 0)

    def prepare(x, carry):
        for h in range(harms):
            a, b = part_a[h, x], part_b[h, x]
            sr, si = source[h, 0, x], source[h, 1, x]
            keep(0, h, x, sr * a + si * b, si * a - sr * b, field_a, 1)
        return carry

    planes(size_x, prepare, 2)

    def send_group(s, g, field):
        for j in range(GROUP):
            h = g * GROUP + j
            for r in range(2):
                x_send[s, 0, h, r] = field[h, r, 1].astype(x_send.dtype)
                x_send[s, 1, h, r] = field[h, r, size_x].astype(x_send.dtype)
        each(lambda axis, side: f_copy(s, g, axis, side, side).start())

    def launch(g, carry):
        send_group(0, g, field_a)
        return carry

    lax.fori_loop(0, groups, launch, 0)

    for s in range(1, SWEEPS):
        old = field_a if s % 2 == 1 else field_b
        final = s == SWEEPS - 1
        new = out_ref if final else (field_b if s % 2 == 1 else field_a)
        pad = 0 if final else 1

        def sweep(g, carry, s=s, old=old, new=new, pad=pad, final=final):
            each(lambda axis, side: f_copy(s - 1, g, axis, 1 - side, side).wait_recv())
            for j in range(GROUP):
                h = g * GROUP + j
                for r in range(2):
                    old[h, r, 0] = x_recv[s - 1, 0, h, r].astype(jnp.float32)
                    old[h, r, size_x + 1] = x_recv[s - 1, 1, h, r].astype(jnp.float32)

            def plane(x, inner):
                faces = [coef[i, x] for i in range(6)]
                for j in range(GROUP):
                    h = g * GROUP + j
                    nums = []
                    for r in range(2):
                        own = old[h, r, x + 1]
                        up, down = shift_y(
                            own,
                            y_recv[s - 1, 0, h, r, pl.ds(x, 1), :],
                            y_recv[s - 1, 1, h, r, pl.ds(x, 1), :],
                        )
                        num = source[h, r, x] + faces[0] * old[h, r, x + 2]
                        num = num + faces[1] * old[h, r, x]
                        num = num + (faces[2] * up + faces[3] * down)
                        num = num + faces[4] * pltpu.roll(own, size_z - 1, 1)
                        num = num + faces[5] * pltpu.roll(own, 1, 1)
                        nums.append(num)
                    a, b = part_a[h, x], part_b[h, x]
                    keep(
                        s, h, x, nums[0] * a + nums[1] * b, nums[1] * a - nums[0] * b, new, pad
                    )
                return inner

            planes(size_x, plane, 4)
            if not final:
                send_group(s, g, new)
            return carry

        lax.fori_loop(0, groups, sweep, 0)

    each(lambda axis, side: c_copy(axis, side, side).wait_send())

    def finish(g, carry):
        for s in range(SWEEPS - 1):
            each(lambda axis, side, s=s: f_copy(s, g, axis, side, side).wait_send())
        return carry

    lax.fori_loop(0, groups, finish, 0)

    def drain(c, carry):
        core_copy(c).wait_send()
        one_copy(c).wait_send()
        two_copy(c).wait_send()
        for hop in range(RADIX - 1):
            z_send(c, hop, lambda copy: copy.wait_send())
        return carry

    lax.fori_loop(0, steps, drain, 0)


def fast_body(wall_temp, owner_map, stencil_column, material, conductivity, capacity):
    steps, patches, _ = wall_temp.shape
    size_x, size_y, size_z = material.shape
    cells = size_x * size_y
    total = cells * lax.axis_size("sx") * lax.axis_size("sy")
    owner = owner_map[:, 0]
    target = ((owner % 2) * (total // 2) + (owner // 2) * cells + stencil_column)[None, :]
    harms = HARM // lax.axis_size("tm")
    groups = harms // GROUP
    table = dft_table().astype(jnp.float32).reshape(HARM, 2, TIME)[:, :, :steps]
    table = lax.dynamic_slice_in_dim(table, lax.axis_index("tm") * harms, harms, 0)
    f32, bf16 = jnp.float32, jnp.bfloat16
    tile = (size_x, size_y, size_z)
    flat = (cells, size_z)
    padded = (harms, 2, size_x + 2, size_y, size_z)
    x_edge = (SWEEPS - 1, 2, harms, 2, size_y, size_z)
    y_edge = (SWEEPS - 1, 2, harms, 2, size_x, size_z)
    shapes = [
        ((total, patches), bf16),
        ((RING, 4) + flat, f32),
        ((steps, 4) + flat, bf16),
        ((steps, 4) + flat, bf16),
        ((RING, 2) + flat, f32),
        ((steps, 2) + flat, bf16),
        ((steps, 2) + flat, bf16),
        ((RING,) + flat, f32),
        ((steps,) + flat, bf16),
        ((steps,) + flat, bf16),
        ((RADIX * steps,) + flat, bf16),
        (tile, f32),
        (tile, f32),
        ((2, size_x, size_z), f32),
        ((2, size_y, size_z), f32),
        ((2, size_x, size_z), f32),
        ((6,) + tile, f32),
        ((harms,) + tile, f32),
        ((harms,) + tile, f32),
        ((harms, 2) + tile, f32),
        (padded, f32),
        (padded, f32),
        (x_edge, bf16),
        (x_edge, bf16),
        (y_edge, f32),
        (y_edge, f32),
    ]
    sems = (
        [(steps,)] * 6
        + [(2, RADIX - 1, steps)] * 2
        + [(2, 2)] * 2
        + [(SWEEPS - 1, groups, 2)] * 4
    )
    counts = {axis: lax.axis_size(axis) for axis in ("sx", "sy")}
    smem = pl.BlockSpec(memory_space=pltpu.SMEM)
    vmem = pl.BlockSpec(memory_space=pltpu.VMEM)
    return pl.pallas_call(
        functools.partial(blade_kernel, counts),
        out_shape=jax.ShapeDtypeStruct((harms, 2) + tile, f32),
        in_specs=[smem] * 4 + [vmem] * 3,
        out_specs=vmem,
        scratch_shapes=[pltpu.VMEM(*shape) for shape in shapes]
        + [pltpu.SemaphoreType.DMA(shape) for shape in sems],
        compiler_params=pltpu.CompilerParams(
            collective_id=1, has_side_effects=True, vmem_limit_bytes=58 * 1024 * 1024
        ),
    )(
        conductivity,
        capacity,
        table[:, 0].reshape(-1),
        table[:, 1].reshape(-1),
        target,
        wall_temp,
        material,
    )


def solution(mesh):
    in_specs = (
        P("tm", ("sx", "sy"), None),
        P(("sx", "sy"), None),
        P(("sx", "sy")),
        P("sx", "sy", None),
        P(),
        P(),
    )
    out_specs = P("tm", None, "sx", "sy", None)
    direct = mesh.shape["tm"] == RADIX and mesh.shape["sx"] == 2 and mesh.shape["sy"] == 4
    step = fast_body if direct else body
    return jax.shard_map(step, mesh=mesh, in_specs=in_specs, out_specs=out_specs, check_vma=False)
```

```python
import functools
import math

import jax
import jax.numpy as jnp
from jax import lax
from jax.experimental import pallas as pl
from jax.experimental.pallas import tpu as pltpu
from jax.sharding import PartitionSpec as P

TIME = 64
HARM = 32
NMAT = 4
SWEEPS = 4


omega_step = 0.1


def with_halo(block, sides, width):
    for axis, dim in sides:
        count = lax.axis_size(axis)
        forward = [(i, i + 1) for i in range(count - 1)]
        backward = [(target, source) for source, target in forward]
        low = lax.ppermute(
            lax.slice_in_dim(block, block.shape[dim] - width, None, axis=dim), axis, forward
        )
        high = lax.ppermute(lax.slice_in_dim(block, 0, width, axis=dim), axis, backward)
        block = jnp.concatenate([low, block, high], axis=dim)
    return block


def dft_table():
    freq_index = jnp.arange(HARM, dtype=jnp.int32)
    time_index = jnp.arange(TIME, dtype=jnp.int32)
    phase_int = freq_index[:, None] * time_index[None, :] % TIME
    angles = phase_int.astype(jnp.float32) * jnp.float32(2.0 * math.pi / TIME)
    amplitude = jnp.float32(2.0 / math.sqrt(TIME))
    table_rows = jnp.stack([amplitude * jnp.cos(angles), -amplitude * jnp.sin(angles)], axis=1)
    return table_rows.reshape(2 * HARM, TIME).astype(jnp.bfloat16)


def lookup(material, table):
    values = jnp.zeros(material.shape, jnp.float32)
    for material_id in range(NMAT):
        values = jnp.where(material == material_id, table[material_id], values)
    return values


def face_value(conduct, other):
    other = jnp.where(other > 0, other, conduct)
    return 2.0 * conduct * other / (conduct + other)


def face_values(conduct, padded):
    next_x = face_value(conduct, padded[2:, 1:-1, 1:-1])
    prev_x = face_value(conduct, padded[:-2, 1:-1, 1:-1])
    next_y = face_value(conduct, padded[1:-1, 2:, 1:-1])
    prev_y = face_value(conduct, padded[1:-1, :-2, 1:-1])
    next_z = face_value(conduct, padded[1:-1, 1:-1, 2:])
    prev_z = face_value(conduct, padded[1:-1, 1:-1, :-2])
    total = next_x + prev_x + next_y + prev_y + next_z + prev_z
    return ((next_x, prev_x, next_y, prev_y, next_z, prev_z), total)


def relax_sweep(padded, source, faces, real_den, imag_den):
    next_x, prev_x, next_y, prev_y, next_z, prev_z = faces
    nearby = next_x * padded[..., 2:, 1:-1, 1:-1] + prev_x * padded[..., :-2, 1:-1, 1:-1]
    nearby = nearby + next_y * padded[..., 1:-1, 2:, 1:-1] + prev_y * padded[..., 1:-1, :-2, 1:-1]
    nearby = nearby + next_z * padded[..., 1:-1, 1:-1, 2:] + prev_z * padded[..., 1:-1, 1:-1, :-2]
    numerator = source + nearby
    real_num = numerator[..., 0, :, :, :]
    imag_num = numerator[..., 1, :, :, :]
    modulus = real_den * real_den + imag_den * imag_den
    real_out = (real_num * real_den + imag_num * imag_den) / modulus
    imag_out = (imag_num * real_den - real_num * imag_den) / modulus
    return jnp.stack([real_out, imag_out], axis=-4)


def to_harmonics(payload):
    transform_rows = dft_table()
    gathered = lax.all_to_all(payload, "tm", split_axis=1, concat_axis=0, tiled=True)
    flattened = gathered.reshape(TIME, gathered.shape[1] * gathered.shape[2])
    harmonic = jnp.dot(transform_rows, flattened, preferred_element_type=jnp.float32)
    harmonic = harmonic.astype(jnp.bfloat16).reshape(2 * HARM, gathered.shape[1], gathered.shape[2])
    return lax.all_to_all(harmonic, "tm", split_axis=0, concat_axis=1, tiled=True)


def to_owners(payload, owner_map, stencil_column):
    owners = lax.axis_size("sx") * lax.axis_size("sy")
    capacity_slots = 2 * payload.shape[1] // owners
    owner_ids = owner_map[:, 0]
    onehot = (owner_ids[:, None] == jnp.arange(owners, dtype=jnp.int32)[None, :]).astype(jnp.int32)
    rank_all = jnp.cumsum(onehot, axis=0) - onehot
    rank_own = jnp.sum(rank_all * onehot, axis=1)
    slot_index = owner_ids * capacity_slots + rank_own
    buffer = jnp.zeros((payload.shape[0], owners * capacity_slots, payload.shape[2]), jnp.bfloat16)
    buffer = buffer.at[:, slot_index, :].set(payload)
    columns = (
        jnp.full((1, owners * capacity_slots), -1, jnp.int32).at[0, slot_index].set(stencil_column)
    )
    return (
        lax.all_to_all(buffer, ("sx", "sy"), split_axis=1, concat_axis=1, tiled=True),
        lax.all_to_all(columns, ("sx", "sy"), split_axis=1, concat_axis=1, tiled=True),
    )


def body(wall_temp, owner_map, stencil_column, material, conductivity, capacity):
    received, columns = to_owners(wall_temp, owner_map, stencil_column)
    harmonic = to_harmonics(received)
    size_x, size_y, size_z = material.shape
    local_harms = harmonic.shape[0] // 2
    column_hits = (jnp.arange(size_x * size_y, dtype=jnp.int32)[:, None] == columns).astype(
        jnp.bfloat16
    )
    source = jnp.einsum("ps,csz->cpz", column_hits, harmonic, preferred_element_type=jnp.float32)
    source = source.reshape(local_harms, 2, size_x, size_y, size_z)
    conduct = lookup(material, conductivity)
    heat_cap = lookup(material, capacity)
    rim = with_halo(conduct.astype(jnp.bfloat16), (("sx", 0), ("sy", 1)), 1).astype(conduct.dtype)
    rim = jnp.pad(rim, ((0, 0), (0, 0), (1, 1)), mode="edge")
    faces, real_den = face_values(conduct, rim)
    harm_index = lax.axis_index("tm") * local_harms + jnp.arange(local_harms, dtype=jnp.int32)
    imag_den = omega_step * harm_index.astype(jnp.float32)[:, None, None, None] * heat_cap
    start = jnp.zeros((local_harms, 2, size_x + 2, size_y + 2, size_z + 2), jnp.float32)
    field = relax_sweep(start, source, faces, real_den, imag_den)
    for sweep in range(SWEEPS - 1):
        padded = with_halo(field, (("sx", 2), ("sy", 3)), 1)
        padded = jnp.pad(padded, ((0, 0), (0, 0), (0, 0), (0, 0), (1, 1)))
        field = relax_sweep(padded, source, faces, real_den, imag_den)
    return field


RADIX = 4
GROUP = 2


def planes(count, body, width):
    def block(i, carry):
        for n in range(width):
            body(i * width + n, 0)
        return carry

    lax.fori_loop(0, count // width, block, 0)


def zero_refs(cond, refs):
    @pl.when(cond)
    def _():
        for ref in refs:
            ref[...] = jnp.zeros(ref.shape, ref.dtype)


LAGS = (1, 3, 5, 8, 11, 14)
FACES_AT = 12
RING = 4


def blade_kernel(
    counts, cond_ref, cap_ref, cos_ref, sin_ref, target_ref, wall_ref, mat_ref, out_ref,
    hits, core_own, core_send, core_recv, one_keep, one_send, one_recv,
    two_keep, two_send, two_recv, rows_ref,
    conduct, heat, cy_send, cx_recv, cy_recv, coef, part_a, part_b, source,
    field_a, field_b, x_send, x_recv, y_send, y_recv,
    core_ssem, core_rsem, one_ssem, one_rsem, two_ssem, two_rsem, z_ssem, z_rsem,
    c_ssem, c_rsem, x_ssem, x_rsem, y_ssem, y_rsem,
):
    steps, patches, _ = wall_ref.shape
    cells = rows_ref.shape[1]
    size_x, size_y, size_z = mat_ref.shape
    harms = source.shape[0]
    groups = harms // GROUP
    tm, sx, sy = (lax.axis_index(axis) for axis in ("tm", "sx", "sy"))
    x, core = sy // 2, sy % 2
    mesh_id = pl.DeviceIdType.MESH
    last = RADIX - 1
    place = {"sx": sx, "sy": sy}
    has = {axis: (place[axis] > 0, place[axis] < counts[axis] - 1) for axis in place}
    beside = {axis: (place[axis] - 1, place[axis] + 1) for axis in place}
    sides = [(axis, side) for axis in ("sx", "sy") for side in (0, 1)]
    inner = jnp.logical_and(has["sy"][0], has["sy"][1])

    barrier = pltpu.get_barrier_semaphore()

    def greet(*peer):
        pl.semaphore_signal(barrier, inc=1, device_id=peer, device_id_type=mesh_id)

    greet(tm, sx, 2 * x + 1 - core)
    greet(tm, sx, 2 * (1 - x) + core)
    greet(tm, 1 - sx, sy)
    pl.when(tm > 0)(lambda: greet(tm - 1, sx, sy))
    pl.when(tm < last)(lambda: greet(tm + 1, sx, sy))
    pl.when(inner)(lambda: greet(tm, sx, 3 - sy))
    expected = 3 + sum(flag.astype(jnp.int32) for flag in (tm > 0, tm < last, inner))

    for axis, (c_buf, f_buf) in {"sx": (cx_recv, x_recv), "sy": (cy_recv, y_recv)}.items():
        for side in (0, 1):
            zero_refs(
                jnp.logical_not(has[axis][side]),
                [c_buf.at[side]] + [f_buf.at[s, side] for s in range(SWEEPS - 1)],
            )

    strip = 64

    def mark(i, carry):
        ids = lax.broadcasted_iota(jnp.int32, (strip, patches), 0) + i * strip
        match = jnp.where(ids == target_ref[...], 1.0, 0.0)
        hits[pl.ds(pl.multiple_of(i * strip, strip), strip), :] = match.astype(jnp.bfloat16)
        return carry

    lax.fori_loop(0, hits.shape[0] // strip, mark, 0)

    def cell_values(x, carry):
        mat = mat_ref[x]
        con = jnp.zeros(mat.shape, jnp.float32)
        cap = jnp.zeros(mat.shape, jnp.float32)
        for m in range(NMAT):
            con = jnp.where(mat == m, cond_ref[m], con)
            cap = jnp.where(mat == m, cap_ref[m], cap)
        conduct[x] = con
        heat[x] = cap
        cy_send[0, pl.ds(x, 1), :] = con[0:1]
        cy_send[1, pl.ds(x, 1), :] = con[size_y - 1 :]
        return carry

    lax.fori_loop(0, size_x, cell_values, 0)

    def clear(h, carry):
        for r in range(2):
            source[h, r] = jnp.zeros((size_x, size_y, size_z), jnp.float32)
        return carry

    lax.fori_loop(0, harms, clear, 0)
    pl.semaphore_wait(barrier, expected)

    def flip(bit, odd):
        return bit + odd - 2 * bit * odd

    def pick(c, u, v):
        turn = c % 2
        cell_x = flip(x, u + turn * (v - u))
        cell_y = flip(sx, v + turn * (u - v))
        return cell_y * 2 + cell_x

    def core_copy(c):
        return pltpu.make_async_remote_copy(
            src_ref=core_send.at[c], dst_ref=core_recv.at[c],
            send_sem=core_ssem.at[c], recv_sem=core_rsem.at[c],
            device_id=(tm, sx, 2 * x + 1 - core), device_id_type=mesh_id,
        )

    def plane_copy(c, send, recv, ssem, rsem, along_y):
        peer = (tm, flip(sx, along_y), 2 * flip(x, 1 - along_y) + core)
        return pltpu.make_async_remote_copy(
            src_ref=send.at[c], dst_ref=recv.at[c], send_sem=ssem.at[c], recv_sem=rsem.at[c],
            device_id=peer, device_id_type=mesh_id,
        )

    def one_copy(c):
        return plane_copy(c, one_send, one_recv, one_ssem, one_rsem, c % 2)

    def two_copy(c):
        return plane_copy(c, two_send, two_recv, two_ssem, two_rsem, 1 - c % 2)

    def z_copy(c, down, block, hop, peer):
        place = block * steps + c
        return pltpu.make_async_remote_copy(
            src_ref=rows_ref.at[place], dst_ref=rows_ref.at[place],
            send_sem=z_ssem.at[down, hop, c], recv_sem=z_rsem.at[down, hop, c],
            device_id=(peer, sx, sy), device_id_type=mesh_id,
        )

    def z_send(c, hop, act):
        @pl.when(jnp.logical_and(tm < last, tm - hop >= 0))
        def _():
            act(z_copy(c, 0, tm - hop, hop, tm + 1))

        @pl.when(jnp.logical_and(tm > 0, tm + hop <= last))
        def _():
            act(z_copy(c, 1, tm + hop, hop, tm - 1))

    def z_arrive(c, hop):
        @pl.when(tm - hop - 1 >= 0)
        def _():
            z_copy(c, 0, tm - hop - 1, hop, tm - 1).wait_recv()

        @pl.when(tm + hop + 1 <= last)
        def _():
            z_copy(c, 1, tm + hop + 1, hop, tm + 1).wait_recv()

    def start(copy):
        copy.start()

    def c_copy(axis, side, toward):
        if axis == "sx":
            src, dst = conduct.at[(size_x - 1) * side], cx_recv.at[1 - side]
        else:
            src, dst = cy_send.at[side], cy_recv.at[1 - side]
        slot = 0 if axis == "sx" else 1
        return pltpu.make_async_remote_copy(
            src_ref=src, dst_ref=dst, send_sem=c_ssem.at[slot, side],
            recv_sem=c_rsem.at[slot, 1 - side],
            device_id={axis: beside[axis][toward]}, device_id_type=pl.DeviceIdType.MESH,
        )

    def f_copy(s, g, axis, side, toward):
        send, recv, ssem, rsem = (
            (x_send, x_recv, x_ssem, x_rsem) if axis == "sx" else (y_send, y_recv, y_ssem, y_rsem)
        )
        part = pl.ds(g * GROUP, GROUP)
        return pltpu.make_async_remote_copy(
            src_ref=send.at[s, side, part], dst_ref=recv.at[s, 1 - side, part],
            send_sem=ssem.at[s, g, side], recv_sem=rsem.at[s, g, 1 - side],
            device_id={axis: beside[axis][toward]}, device_id_type=pl.DeviceIdType.MESH,
        )

    def each(fn):
        for axis, side in sides:

            @pl.when(has[axis][side])
            def _(axis=axis, side=side):
                fn(axis, side)

    each(lambda axis, side: c_copy(axis, side, side).start())

    first = (lax.axis_index("tm") * harms).astype(jnp.float32)
    row = lax.broadcasted_iota(jnp.int32, (size_y, size_z), 0)
    lane = lax.broadcasted_iota(jnp.int32, (size_y, size_z), 1)

    def shift_y(value, low, high):
        up = jnp.where(row == size_y - 1, high, pltpu.roll(value, size_y - 1, 0))
        down = jnp.where(row == 0, low, pltpu.roll(value, 1, 0))
        return up, down

    def keep(s, h, x, real, imag, dst, pad):
        for r, value in enumerate((real, imag)):
            dst[h, r, x + pad] = value
            if s < SWEEPS - 1:
                y_send[s, 0, h, r, pl.ds(x, 1), :] = value[0:1]
                y_send[s, 1, h, r, pl.ds(x, 1), :] = value[size_y - 1 :]

    def set_faces(x, carry):
        own = conduct[x]
        above = jnp.where(x == size_x - 1, cx_recv[1], conduct[jnp.minimum(x + 1, size_x - 1)])
        below = jnp.where(x == 0, cx_recv[0], conduct[jnp.maximum(x - 1, 0)])
        up, down = shift_y(own, cy_recv[0, pl.ds(x, 1), :], cy_recv[1, pl.ds(x, 1), :])
        right = jnp.where(lane == size_z - 1, own, pltpu.roll(own, size_z - 1, 1))
        left = jnp.where(lane == 0, own, pltpu.roll(own, 1, 1))
        total = None
        for i, other in enumerate((above, below, up, down, right, left)):
            face = face_value(own, other)
            total = face if total is None else total + face
            if i == 4:
                face = jnp.where(lane == size_z - 1, 0.0, face)
            if i == 5:
                face = jnp.where(lane == 0, 0.0, face)
            coef[i, x] = face
        cap = heat[x]
        for h in range(harms):
            imag_den = (omega_step * (first + h)) * cap
            inverse = 1.0 / (total * total + imag_den * imag_den)
            a, b = total * inverse, imag_den * inverse
            part_a[h, x] = a
            part_b[h, x] = b
        return carry

    def for_partner(c):
        pair = jnp.concatenate([wall_ref[c], wall_ref[c + 1]], axis=1)

        def sums(own_core):
            rows = pl.ds(pl.multiple_of(own_core * (4 * cells), 4 * cells), 4 * cells)
            return jnp.dot(hits[rows, :], pair, preferred_element_type=jnp.float32)

        sent = sums(1 - core).astype(jnp.bfloat16)
        for n in range(2):
            core_send[c + n] = sent[:, n * size_z : (n + 1) * size_z].reshape(4, cells, size_z)
            core_copy(c + n).start()
        kept = sums(core)
        for n in range(2):
            core_own[(c + n) % RING] = kept[:, n * size_z : (n + 1) * size_z].reshape(
                4, cells, size_z
            )

    def first_turn(c):
        core_copy(c).wait_recv()
        for u in (1, 0):
            for v in range(2):
                tile = pick(c, u, v)
                both = core_own[c % RING, tile] + core_recv[c, tile].astype(jnp.float32)
                if u == 1:
                    one_send[c, v] = both.astype(jnp.bfloat16)
                else:
                    one_keep[c % RING, v] = both
            if u == 1:
                one_copy(c).start()

    def second_turn(c):
        one_copy(c).wait_recv()
        two_send[c] = (one_keep[c % RING, 1] + one_recv[c, 1].astype(jnp.float32)).astype(
            jnp.bfloat16
        )
        two_copy(c).start()
        two_keep[c % RING] = one_keep[c % RING, 0] + one_recv[c, 0].astype(jnp.float32)

    def complete(c):
        two_copy(c).wait_recv()
        total = two_keep[c % RING] + two_recv[c].astype(jnp.float32)
        rows_ref[tm * steps + c] = total.astype(jnp.bfloat16)
        z_send(c, 0, start)

    def hop_one(c):
        z_arrive(c, 0)
        z_send(c, 1, start)

    def hop_two(c):
        z_arrive(c, 1)
        z_send(c, 2, start)

    def transform(c):
        def plane(x, carry):
            span = pl.ds(pl.multiple_of(x * size_y, size_y), size_y)
            folded = []
            for b in (c - 1, c):
                t0, t1, t2, t3 = [
                    rows_ref[a * steps + b, span, :].astype(jnp.float32) for a in range(RADIX)
                ]
                even, odd = t0 + t2, t1 + t3
                turn_r, turn_i = t0 - t2, t3 - t1
                folded.append(
                    ((even + odd, None), (turn_r, turn_i), (even - odd, None), (turn_r, -turn_i))
                )
            for j in range(harms):
                real, imag = source[j, 0, x], source[j, 1, x]
                for n, b in enumerate((c - 1, c)):
                    co, si = cos_ref[j * steps + b], sin_ref[j * steps + b]
                    fr, fi = folded[n][j % RADIX]
                    real = real + co * fr
                    imag = imag + si * fr
                    if fi is not None:
                        real = real - si * fi
                        imag = imag + co * fi
                source[j, 0, x] = real
                source[j, 1, x] = imag
            return carry

        planes(size_x, plane, 2)

    def hop_three(c):
        z_arrive(c, 2)
        pl.when(c % 2 == 1)(lambda: transform(c))

    stages = (first_turn, second_turn, complete, hop_one, hop_two, hop_three)

    def at(i, lag, stage):
        live = jnp.logical_and(i >= lag, i < steps + lag)
        pl.when(live)(lambda: stage(i - lag))

    def tick(i, carry):
        for lag, stage in reversed(list(zip(LAGS[:-1], stages[:-1]))):
            at(i, lag, stage)
        pl.when(jnp.logical_and(i % 2 == 0, i < steps))(lambda: for_partner(i))

        @pl.when(i == FACES_AT)
        def _():
            each(lambda axis, side: c_copy(axis, 1 - side, side).wait_recv())
            planes(size_x, set_faces, 2)

        at(i, LAGS[-1], hop_three)
        return carry

    lax.fori_loop(0, steps + LAGS[-1], tick, 0)

    def prepare(x, carry):
        for h in range(harms):
            a, b = part_a[h, x], part_b[h, x]
            sr, si = source[h, 0, x], source[h, 1, x]
            keep(0, h, x, sr * a + si * b, si * a - sr * b, field_a, 1)
        return carry

    planes(size_x, prepare, 2)

    def send_group(s, g, field):
        for j in range(GROUP):
            h = g * GROUP + j
            for r in range(2):
                x_send[s, 0, h, r] = field[h, r, 1].astype(x_send.dtype)
                x_send[s, 1, h, r] = field[h, r, size_x].astype(x_send.dtype)
        each(lambda axis, side: f_copy(s, g, axis, side, side).start())

    def launch(g, carry):
        send_group(0, g, field_a)
        return carry

    lax.fori_loop(0, groups, launch, 0)

    for s in range(1, SWEEPS):
        old = field_a if s % 2 == 1 else field_b
        final = s == SWEEPS - 1
        new = out_ref if final else (field_b if s % 2 == 1 else field_a)
        pad = 0 if final else 1

        def sweep(g, carry, s=s, old=old, new=new, pad=pad, final=final):
            each(lambda axis, side: f_copy(s - 1, g, axis, 1 - side, side).wait_recv())
            for j in range(GROUP):
                h = g * GROUP + j
                for r in range(2):
                    old[h, r, 0] = x_recv[s - 1, 0, h, r].astype(jnp.float32)
                    old[h, r, size_x + 1] = x_recv[s - 1, 1, h, r].astype(jnp.float32)

            def plane(x, inner):
                faces = [coef[i, x] for i in range(6)]
                for j in range(GROUP):
                    h = g * GROUP + j
                    nums = []
                    for r in range(2):
                        own = old[h, r, x + 1]
                        up, down = shift_y(
                            own,
                            y_recv[s - 1, 0, h, r, pl.ds(x, 1), :],
                            y_recv[s - 1, 1, h, r, pl.ds(x, 1), :],
                        )
                        num = source[h, r, x] + faces[0] * old[h, r, x + 2]
                        num = num + faces[1] * old[h, r, x]
                        num = num + (faces[2] * up + faces[3] * down)
                        num = num + faces[4] * pltpu.roll(own, size_z - 1, 1)
                        num = num + faces[5] * pltpu.roll(own, 1, 1)
                        nums.append(num)
                    a, b = part_a[h, x], part_b[h, x]
                    keep(
                        s, h, x, nums[0] * a + nums[1] * b, nums[1] * a - nums[0] * b, new, pad
                    )
                return inner

            planes(size_x, plane, 4)
            if not final:
                send_group(s, g, new)
            return carry

        lax.fori_loop(0, groups, sweep, 0)

    each(lambda axis, side: c_copy(axis, side, side).wait_send())

    def finish(g, carry):
        for s in range(SWEEPS - 1):
            each(lambda axis, side, s=s: f_copy(s, g, axis, side, side).wait_send())
        return carry

    lax.fori_loop(0, groups, finish, 0)

    def drain(c, carry):
        core_copy(c).wait_send()
        one_copy(c).wait_send()
        two_copy(c).wait_send()
        for hop in range(RADIX - 1):
            z_send(c, hop, lambda copy: copy.wait_send())
        return carry

    lax.fori_loop(0, steps, drain, 0)


def fast_body(wall_temp, owner_map, stencil_column, material, conductivity, capacity):
    steps, patches, _ = wall_temp.shape
    size_x, size_y, size_z = material.shape
    cells = size_x * size_y
    total = cells * lax.axis_size("sx") * lax.axis_size("sy")
    owner = owner_map[:, 0]
    target = ((owner % 2) * (total // 2) + (owner // 2) * cells + stencil_column)[None, :]
    harms = HARM // lax.axis_size("tm")
    groups = harms // GROUP
    table = dft_table().astype(jnp.float32).reshape(HARM, 2, TIME)[:, :, :steps]
    table = lax.dynamic_slice_in_dim(table, lax.axis_index("tm") * harms, harms, 0)
    f32, bf16 = jnp.float32, jnp.bfloat16
    tile = (size_x, size_y, size_z)
    flat = (cells, size_z)
    padded = (harms, 2, size_x + 2, size_y, size_z)
    x_edge = (SWEEPS - 1, 2, harms, 2, size_y, size_z)
    y_edge = (SWEEPS - 1, 2, harms, 2, size_x, size_z)
    shapes = [
        ((total, patches), bf16),
        ((RING, 4) + flat, f32),
        ((steps, 4) + flat, bf16),
        ((steps, 4) + flat, bf16),
        ((RING, 2) + flat, f32),
        ((steps, 2) + flat, bf16),
        ((steps, 2) + flat, bf16),
        ((RING,) + flat, f32),
        ((steps,) + flat, bf16),
        ((steps,) + flat, bf16),
        ((RADIX * steps,) + flat, bf16),
        (tile, f32),
        (tile, f32),
        ((2, size_x, size_z), f32),
        ((2, size_y, size_z), f32),
        ((2, size_x, size_z), f32),
        ((6,) + tile, f32),
        ((harms,) + tile, f32),
        ((harms,) + tile, f32),
        ((harms, 2) + tile, f32),
        (padded, f32),
        (padded, f32),
        (x_edge, bf16),
        (x_edge, bf16),
        (y_edge, f32),
        (y_edge, f32),
    ]
    sems = (
        [(steps,)] * 6
        + [(2, RADIX - 1, steps)] * 2
        + [(2, 2)] * 2
        + [(SWEEPS - 1, groups, 2)] * 4
    )
    counts = {axis: lax.axis_size(axis) for axis in ("sx", "sy")}
    smem = pl.BlockSpec(memory_space=pltpu.SMEM)
    vmem = pl.BlockSpec(memory_space=pltpu.VMEM)
    return pl.pallas_call(
        functools.partial(blade_kernel, counts),
        out_shape=jax.ShapeDtypeStruct((harms, 2) + tile, f32),
        in_specs=[smem] * 4 + [vmem] * 3,
        out_specs=vmem,
        scratch_shapes=[pltpu.VMEM(*shape) for shape in shapes]
        + [pltpu.SemaphoreType.DMA(shape) for shape in sems],
        compiler_params=pltpu.CompilerParams(
            collective_id=1, has_side_effects=True, vmem_limit_bytes=58 * 1024 * 1024
        ),
    )(
        conductivity,
        capacity,
        table[:, 0].reshape(-1),
        table[:, 1].reshape(-1),
        target,
        wall_temp,
        material,
    )


def solution(mesh):
    in_specs = (
        P("tm", ("sx", "sy"), None),
        P(("sx", "sy"), None),
        P(("sx", "sy")),
        P("sx", "sy", None),
        P(),
        P(),
    )
    out_specs = P("tm", None, "sx", "sy", None)
    direct = mesh.shape["tm"] == RADIX and mesh.shape["sx"] == 2 and mesh.shape["sy"] == 4
    step = fast_body if direct else body
    return jax.shard_map(step, mesh=mesh, in_specs=in_specs, out_specs=out_specs, check_vma=False)
```

```python
import functools
import math

import jax
import jax.numpy as jnp
from jax import lax
from jax.experimental import pallas as pl
from jax.experimental.pallas import tpu as pltpu
from jax.sharding import PartitionSpec as P

TIME = 64
HARM = 32
NMAT = 4
SWEEPS = 4


omega_step = 0.1


def with_halo(block, sides, width):
    for axis, dim in sides:
        count = lax.axis_size(axis)
        forward = [(i, i + 1) for i in range(count - 1)]
        backward = [(target, source) for source, target in forward]
        low = lax.ppermute(
            lax.slice_in_dim(block, block.shape[dim] - width, None, axis=dim), axis, forward
        )
        high = lax.ppermute(lax.slice_in_dim(block, 0, width, axis=dim), axis, backward)
        block = jnp.concatenate([low, block, high], axis=dim)
    return block


def dft_table():
    freq_index = jnp.arange(HARM, dtype=jnp.int32)
    time_index = jnp.arange(TIME, dtype=jnp.int32)
    phase_int = freq_index[:, None] * time_index[None, :] % TIME
    angles = phase_int.astype(jnp.float32) * jnp.float32(2.0 * math.pi / TIME)
    amplitude = jnp.float32(2.0 / math.sqrt(TIME))
    table_rows = jnp.stack([amplitude * jnp.cos(angles), -amplitude * jnp.sin(angles)], axis=1)
    return table_rows.reshape(2 * HARM, TIME).astype(jnp.bfloat16)


def lookup(material, table):
    values = jnp.zeros(material.shape, jnp.float32)
    for material_id in range(NMAT):
        values = jnp.where(material == material_id, table[material_id], values)
    return values


def face_value(conduct, other):
    other = jnp.where(other > 0, other, conduct)
    return 2.0 * conduct * other / (conduct + other)


def face_values(conduct, padded):
    next_x = face_value(conduct, padded[2:, 1:-1, 1:-1])
    prev_x = face_value(conduct, padded[:-2, 1:-1, 1:-1])
    next_y = face_value(conduct, padded[1:-1, 2:, 1:-1])
    prev_y = face_value(conduct, padded[1:-1, :-2, 1:-1])
    next_z = face_value(conduct, padded[1:-1, 1:-1, 2:])
    prev_z = face_value(conduct, padded[1:-1, 1:-1, :-2])
    total = next_x + prev_x + next_y + prev_y + next_z + prev_z
    return ((next_x, prev_x, next_y, prev_y, next_z, prev_z), total)


def relax_sweep(padded, source, faces, real_den, imag_den):
    next_x, prev_x, next_y, prev_y, next_z, prev_z = faces
    nearby = next_x * padded[..., 2:, 1:-1, 1:-1] + prev_x * padded[..., :-2, 1:-1, 1:-1]
    nearby = nearby + next_y * padded[..., 1:-1, 2:, 1:-1] + prev_y * padded[..., 1:-1, :-2, 1:-1]
    nearby = nearby + next_z * padded[..., 1:-1, 1:-1, 2:] + prev_z * padded[..., 1:-1, 1:-1, :-2]
    numerator = source + nearby
    real_num = numerator[..., 0, :, :, :]
    imag_num = numerator[..., 1, :, :, :]
    modulus = real_den * real_den + imag_den * imag_den
    real_out = (real_num * real_den + imag_num * imag_den) / modulus
    imag_out = (imag_num * real_den - real_num * imag_den) / modulus
    return jnp.stack([real_out, imag_out], axis=-4)


def to_harmonics(payload):
    transform_rows = dft_table()
    gathered = lax.all_to_all(payload, "tm", split_axis=1, concat_axis=0, tiled=True)
    flattened = gathered.reshape(TIME, gathered.shape[1] * gathered.shape[2])
    harmonic = jnp.dot(transform_rows, flattened, preferred_element_type=jnp.float32)
    harmonic = harmonic.astype(jnp.bfloat16).reshape(2 * HARM, gathered.shape[1], gathered.shape[2])
    return lax.all_to_all(harmonic, "tm", split_axis=0, concat_axis=1, tiled=True)


def to_owners(payload, owner_map, stencil_column):
    owners = lax.axis_size("sx") * lax.axis_size("sy")
    capacity_slots = 2 * payload.shape[1] // owners
    owner_ids = owner_map[:, 0]
    onehot = (owner_ids[:, None] == jnp.arange(owners, dtype=jnp.int32)[None, :]).astype(jnp.int32)
    rank_all = jnp.cumsum(onehot, axis=0) - onehot
    rank_own = jnp.sum(rank_all * onehot, axis=1)
    slot_index = owner_ids * capacity_slots + rank_own
    buffer = jnp.zeros((payload.shape[0], owners * capacity_slots, payload.shape[2]), jnp.bfloat16)
    buffer = buffer.at[:, slot_index, :].set(payload)
    columns = (
        jnp.full((1, owners * capacity_slots), -1, jnp.int32).at[0, slot_index].set(stencil_column)
    )
    return (
        lax.all_to_all(buffer, ("sx", "sy"), split_axis=1, concat_axis=1, tiled=True),
        lax.all_to_all(columns, ("sx", "sy"), split_axis=1, concat_axis=1, tiled=True),
    )


def body(wall_temp, owner_map, stencil_column, material, conductivity, capacity):
    received, columns = to_owners(wall_temp, owner_map, stencil_column)
    harmonic = to_harmonics(received)
    size_x, size_y, size_z = material.shape
    local_harms = harmonic.shape[0] // 2
    column_hits = (jnp.arange(size_x * size_y, dtype=jnp.int32)[:, None] == columns).astype(
        jnp.bfloat16
    )
    source = jnp.einsum("ps,csz->cpz", column_hits, harmonic, preferred_element_type=jnp.float32)
    source = source.reshape(local_harms, 2, size_x, size_y, size_z)
    conduct = lookup(material, conductivity)
    heat_cap = lookup(material, capacity)
    rim = with_halo(conduct.astype(jnp.bfloat16), (("sx", 0), ("sy", 1)), 1).astype(conduct.dtype)
    rim = jnp.pad(rim, ((0, 0), (0, 0), (1, 1)), mode="edge")
    faces, real_den = face_values(conduct, rim)
    harm_index = lax.axis_index("tm") * local_harms + jnp.arange(local_harms, dtype=jnp.int32)
    imag_den = omega_step * harm_index.astype(jnp.float32)[:, None, None, None] * heat_cap
    start = jnp.zeros((local_harms, 2, size_x + 2, size_y + 2, size_z + 2), jnp.float32)
    field = relax_sweep(start, source, faces, real_den, imag_den)
    for sweep in range(SWEEPS - 1):
        padded = with_halo(field, (("sx", 2), ("sy", 3)), 1)
        padded = jnp.pad(padded, ((0, 0), (0, 0), (0, 0), (0, 0), (1, 1)))
        field = relax_sweep(padded, source, faces, real_den, imag_den)
    return field


RADIX = 4
GROUP = 2


def planes(count, body, width):
    def block(i, carry):
        for n in range(width):
            body(i * width + n, 0)
        return carry

    lax.fori_loop(0, count // width, block, 0)


def zero_refs(cond, refs):
    @pl.when(cond)
    def _():
        for ref in refs:
            ref[...] = jnp.zeros(ref.shape, ref.dtype)


LAGS = (1, 3, 4, 7, 10, 13)
FACES_AT = 12
RING = 4


def blade_kernel(
    counts, cond_ref, cap_ref, cos_ref, sin_ref, target_ref, wall_ref, mat_ref, out_ref,
    hits, core_own, core_send, core_recv, one_keep, one_send, one_recv,
    two_keep, two_send, two_recv, rows_ref,
    conduct, heat, cy_send, cx_recv, cy_recv, coef, part_a, part_b, source,
    field_a, field_b, x_send, x_recv, y_send, y_recv,
    core_ssem, core_rsem, one_ssem, one_rsem, two_ssem, two_rsem, z_ssem, z_rsem,
    c_ssem, c_rsem, x_ssem, x_rsem, y_ssem, y_rsem,
):
    steps, patches, _ = wall_ref.shape
    cells = rows_ref.shape[1]
    size_x, size_y, size_z = mat_ref.shape
    harms = source.shape[0]
    groups = harms // GROUP
    tm, sx, sy = (lax.axis_index(axis) for axis in ("tm", "sx", "sy"))
    x, core = sy // 2, sy % 2
    mesh_id = pl.DeviceIdType.MESH
    last = RADIX - 1
    place = {"sx": sx, "sy": sy}
    has = {axis: (place[axis] > 0, place[axis] < counts[axis] - 1) for axis in place}
    beside = {axis: (place[axis] - 1, place[axis] + 1) for axis in place}
    sides = [(axis, side) for axis in ("sx", "sy") for side in (0, 1)]
    inner = jnp.logical_and(has["sy"][0], has["sy"][1])

    barrier = pltpu.get_barrier_semaphore()

    def greet(*peer):
        pl.semaphore_signal(barrier, inc=1, device_id=peer, device_id_type=mesh_id)

    greet(tm, sx, 2 * x + 1 - core)
    greet(tm, sx, 2 * (1 - x) + core)
    greet(tm, 1 - sx, sy)
    pl.when(tm > 0)(lambda: greet(tm - 1, sx, sy))
    pl.when(tm < last)(lambda: greet(tm + 1, sx, sy))
    pl.when(inner)(lambda: greet(tm, sx, 3 - sy))
    expected = 3 + sum(flag.astype(jnp.int32) for flag in (tm > 0, tm < last, inner))

    for axis, (c_buf, f_buf) in {"sx": (cx_recv, x_recv), "sy": (cy_recv, y_recv)}.items():
        for side in (0, 1):
            zero_refs(
                jnp.logical_not(has[axis][side]),
                [c_buf.at[side]] + [f_buf.at[s, side] for s in range(SWEEPS - 1)],
            )

    strip = 64

    def mark(i, carry):
        ids = lax.broadcasted_iota(jnp.int32, (strip, patches), 0) + i * strip
        match = jnp.where(ids == target_ref[...], 1.0, 0.0)
        hits[pl.ds(pl.multiple_of(i * strip, strip), strip), :] = match.astype(jnp.bfloat16)
        return carry

    lax.fori_loop(0, hits.shape[0] // strip, mark, 0)

    def cell_values(x, carry):
        mat = mat_ref[x]
        con = jnp.zeros(mat.shape, jnp.float32)
        cap = jnp.zeros(mat.shape, jnp.float32)
        for m in range(NMAT):
            con = jnp.where(mat == m, cond_ref[m], con)
            cap = jnp.where(mat == m, cap_ref[m], cap)
        conduct[x] = con
        heat[x] = cap
        cy_send[0, pl.ds(x, 1), :] = con[0:1]
        cy_send[1, pl.ds(x, 1), :] = con[size_y - 1 :]
        return carry

    lax.fori_loop(0, size_x, cell_values, 0)

    def clear(h, carry):
        for r in range(2):
            source[h, r] = jnp.zeros((size_x, size_y, size_z), jnp.float32)
        return carry

    lax.fori_loop(0, harms, clear, 0)
    pl.semaphore_wait(barrier, expected)

    def flip(bit, odd):
        return bit + odd - 2 * bit * odd

    def pick(c, u, v):
        turn = c % 2
        cell_x = flip(x, u + turn * (v - u))
        cell_y = flip(sx, v + turn * (u - v))
        return cell_y * 2 + cell_x

    def core_copy(c):
        return pltpu.make_async_remote_copy(
            src_ref=core_send.at[c], dst_ref=core_recv.at[c],
            send_sem=core_ssem.at[c], recv_sem=core_rsem.at[c],
            device_id=(tm, sx, 2 * x + 1 - core), device_id_type=mesh_id,
        )

    def plane_copy(c, send, recv, ssem, rsem, along_y):
        peer = (tm, flip(sx, along_y), 2 * flip(x, 1 - along_y) + core)
        return pltpu.make_async_remote_copy(
            src_ref=send.at[c], dst_ref=recv.at[c], send_sem=ssem.at[c], recv_sem=rsem.at[c],
            device_id=peer, device_id_type=mesh_id,
        )

    def one_copy(c):
        return plane_copy(c, one_send, one_recv, one_ssem, one_rsem, c % 2)

    def two_copy(c):
        return plane_copy(c, two_send, two_recv, two_ssem, two_rsem, 1 - c % 2)

    def z_copy(c, down, block, hop, peer):
        place = block * steps + c
        return pltpu.make_async_remote_copy(
            src_ref=rows_ref.at[place], dst_ref=rows_ref.at[place],
            send_sem=z_ssem.at[down, hop, c], recv_sem=z_rsem.at[down, hop, c],
            device_id=(peer, sx, sy), device_id_type=mesh_id,
        )

    def z_send(c, hop, act):
        @pl.when(jnp.logical_and(tm < last, tm - hop >= 0))
        def _():
            act(z_copy(c, 0, tm - hop, hop, tm + 1))

        @pl.when(jnp.logical_and(tm > 0, tm + hop <= last))
        def _():
            act(z_copy(c, 1, tm + hop, hop, tm - 1))

    def z_arrive(c, hop):
        @pl.when(tm - hop - 1 >= 0)
        def _():
            z_copy(c, 0, tm - hop - 1, hop, tm - 1).wait_recv()

        @pl.when(tm + hop + 1 <= last)
        def _():
            z_copy(c, 1, tm + hop + 1, hop, tm + 1).wait_recv()

    def start(copy):
        copy.start()

    def c_copy(axis, side, toward):
        if axis == "sx":
            src, dst = conduct.at[(size_x - 1) * side], cx_recv.at[1 - side]
        else:
            src, dst = cy_send.at[side], cy_recv.at[1 - side]
        slot = 0 if axis == "sx" else 1
        return pltpu.make_async_remote_copy(
            src_ref=src, dst_ref=dst, send_sem=c_ssem.at[slot, side],
            recv_sem=c_rsem.at[slot, 1 - side],
            device_id={axis: beside[axis][toward]}, device_id_type=pl.DeviceIdType.MESH,
        )

    def f_copy(s, g, axis, side, toward):
        send, recv, ssem, rsem = (
            (x_send, x_recv, x_ssem, x_rsem) if axis == "sx" else (y_send, y_recv, y_ssem, y_rsem)
        )
        part = pl.ds(g * GROUP, GROUP)
        return pltpu.make_async_remote_copy(
            src_ref=send.at[s, side, part], dst_ref=recv.at[s, 1 - side, part],
            send_sem=ssem.at[s, g, side], recv_sem=rsem.at[s, g, 1 - side],
            device_id={axis: beside[axis][toward]}, device_id_type=pl.DeviceIdType.MESH,
        )

    def each(fn):
        for axis, side in sides:

            @pl.when(has[axis][side])
            def _(axis=axis, side=side):
                fn(axis, side)

    each(lambda axis, side: c_copy(axis, side, side).start())

    first = (lax.axis_index("tm") * harms).astype(jnp.float32)
    row = lax.broadcasted_iota(jnp.int32, (size_y, size_z), 0)
    lane = lax.broadcasted_iota(jnp.int32, (size_y, size_z), 1)

    def shift_y(value, low, high):
        up = jnp.where(row == size_y - 1, high, pltpu.roll(value, size_y - 1, 0))
        down = jnp.where(row == 0, low, pltpu.roll(value, 1, 0))
        return up, down

    def keep(s, h, x, real, imag, dst, pad):
        for r, value in enumerate((real, imag)):
            dst[h, r, x + pad] = value
            if s < SWEEPS - 1:
                y_send[s, 0, h, r, pl.ds(x, 1), :] = value[0:1]
                y_send[s, 1, h, r, pl.ds(x, 1), :] = value[size_y - 1 :]

    def set_faces(x, carry):
        own = conduct[x]
        above = jnp.where(x == size_x - 1, cx_recv[1], conduct[jnp.minimum(x + 1, size_x - 1)])
        below = jnp.where(x == 0, cx_recv[0], conduct[jnp.maximum(x - 1, 0)])
        up, down = shift_y(own, cy_recv[0, pl.ds(x, 1), :], cy_recv[1, pl.ds(x, 1), :])
        right = jnp.where(lane == size_z - 1, own, pltpu.roll(own, size_z - 1, 1))
        left = jnp.where(lane == 0, own, pltpu.roll(own, 1, 1))
        total = None
        for i, other in enumerate((above, below, up, down, right, left)):
            face = face_value(own, other)
            total = face if total is None else total + face
            if i == 4:
                face = jnp.where(lane == size_z - 1, 0.0, face)
            if i == 5:
                face = jnp.where(lane == 0, 0.0, face)
            coef[i, x] = face
        cap = heat[x]
        for h in range(harms):
            imag_den = (omega_step * (first + h)) * cap
            inverse = 1.0 / (total * total + imag_den * imag_den)
            a, b = total * inverse, imag_den * inverse
            part_a[h, x] = a
            part_b[h, x] = b
        return carry

    def for_partner(c):
        pair = jnp.concatenate([wall_ref[c], wall_ref[c + 1]], axis=1)

        def sums(own_core):
            rows = pl.ds(pl.multiple_of(own_core * (4 * cells), 4 * cells), 4 * cells)
            return jnp.dot(hits[rows, :], pair, preferred_element_type=jnp.float32)

        sent = sums(1 - core).astype(jnp.bfloat16)
        for n in range(2):
            core_send[c + n] = sent[:, n * size_z : (n + 1) * size_z].reshape(4, cells, size_z)
            core_copy(c + n).start()
        kept = sums(core)
        for n in range(2):
            core_own[(c + n) % RING] = kept[:, n * size_z : (n + 1) * size_z].reshape(
                4, cells, size_z
            )

    def first_turn(c):
        core_copy(c).wait_recv()
        for u in (1, 0):
            for v in range(2):
                tile = pick(c, u, v)
                both = core_own[c % RING, tile] + core_recv[c, tile].astype(jnp.float32)
                if u == 1:
                    one_send[c, v] = both.astype(jnp.bfloat16)
                else:
                    one_keep[c % RING, v] = both
            if u == 1:
                one_copy(c).start()

    def second_turn(c):
        one_copy(c).wait_recv()
        two_send[c] = (one_keep[c % RING, 1] + one_recv[c, 1].astype(jnp.float32)).astype(
            jnp.bfloat16
        )
        two_copy(c).start()
        two_keep[c % RING] = one_keep[c % RING, 0] + one_recv[c, 0].astype(jnp.float32)

    def complete(c):
        two_copy(c).wait_recv()
        total = two_keep[c % RING] + two_recv[c].astype(jnp.float32)
        rows_ref[tm * steps + c] = total.astype(jnp.bfloat16)
        z_send(c, 0, start)

    def hop_one(c):
        z_arrive(c, 0)
        z_send(c, 1, start)

    def hop_two(c):
        z_arrive(c, 1)
        z_send(c, 2, start)

    def transform(c):
        def plane(x, carry):
            span = pl.ds(pl.multiple_of(x * size_y, size_y), size_y)
            folded = []
            for b in (c - 1, c):
                t0, t1, t2, t3 = [
                    rows_ref[a * steps + b, span, :].astype(jnp.float32) for a in range(RADIX)
                ]
                even, odd = t0 + t2, t1 + t3
                turn_r, turn_i = t0 - t2, t3 - t1
                folded.append(
                    ((even + odd, None), (turn_r, turn_i), (even - odd, None), (turn_r, -turn_i))
                )
            for j in range(harms):
                real, imag = source[j, 0, x], source[j, 1, x]
                for n, b in enumerate((c - 1, c)):
                    co, si = cos_ref[j * steps + b], sin_ref[j * steps + b]
                    fr, fi = folded[n][j % RADIX]
                    real = real + co * fr
                    imag = imag + si * fr
                    if fi is not None:
                        real = real - si * fi
                        imag = imag + co * fi
                source[j, 0, x] = real
                source[j, 1, x] = imag
            return carry

        planes(size_x, plane, 2)

    def hop_three(c):
        z_arrive(c, 2)
        pl.when(c % 2 == 1)(lambda: transform(c))

    stages = (first_turn, second_turn, complete, hop_one, hop_two, hop_three)

    def at(i, lag, stage):
        live = jnp.logical_and(i >= lag, i < steps + lag)
        pl.when(live)(lambda: stage(i - lag))

    def tick(i, carry):
        for lag, stage in reversed(list(zip(LAGS[:-1], stages[:-1]))):
            at(i, lag, stage)
        pl.when(jnp.logical_and(i % 2 == 0, i < steps))(lambda: for_partner(i))

        @pl.when(i == FACES_AT)
        def _():
            each(lambda axis, side: c_copy(axis, 1 - side, side).wait_recv())
            planes(size_x, set_faces, 2)

        at(i, LAGS[-1], hop_three)
        return carry

    lax.fori_loop(0, steps + LAGS[-1], tick, 0)

    def prepare(x, carry):
        for h in range(harms):
            a, b = part_a[h, x], part_b[h, x]
            sr, si = source[h, 0, x], source[h, 1, x]
            keep(0, h, x, sr * a + si * b, si * a - sr * b, field_a, 1)
        return carry

    planes(size_x, prepare, 2)

    def send_group(s, g, field):
        for j in range(GROUP):
            h = g * GROUP + j
            for r in range(2):
                x_send[s, 0, h, r] = field[h, r, 1].astype(x_send.dtype)
                x_send[s, 1, h, r] = field[h, r, size_x].astype(x_send.dtype)
        each(lambda axis, side: f_copy(s, g, axis, side, side).start())

    def launch(g, carry):
        send_group(0, g, field_a)
        return carry

    lax.fori_loop(0, groups, launch, 0)

    for s in range(1, SWEEPS):
        old = field_a if s % 2 == 1 else field_b
        final = s == SWEEPS - 1
        new = out_ref if final else (field_b if s % 2 == 1 else field_a)
        pad = 0 if final else 1

        def sweep(g, carry, s=s, old=old, new=new, pad=pad, final=final):
            each(lambda axis, side: f_copy(s - 1, g, axis, 1 - side, side).wait_recv())
            for j in range(GROUP):
                h = g * GROUP + j
                for r in range(2):
                    old[h, r, 0] = x_recv[s - 1, 0, h, r].astype(jnp.float32)
                    old[h, r, size_x + 1] = x_recv[s - 1, 1, h, r].astype(jnp.float32)

            def plane(x, inner):
                faces = [coef[i, x] for i in range(6)]
                for j in range(GROUP):
                    h = g * GROUP + j
                    nums = []
                    for r in range(2):
                        own = old[h, r, x + 1]
                        up, down = shift_y(
                            own,
                            y_recv[s - 1, 0, h, r, pl.ds(x, 1), :],
                            y_recv[s - 1, 1, h, r, pl.ds(x, 1), :],
                        )
                        num = source[h, r, x] + faces[0] * old[h, r, x + 2]
                        num = num + faces[1] * old[h, r, x]
                        num = num + (faces[2] * up + faces[3] * down)
                        num = num + faces[4] * pltpu.roll(own, size_z - 1, 1)
                        num = num + faces[5] * pltpu.roll(own, 1, 1)
                        nums.append(num)
                    a, b = part_a[h, x], part_b[h, x]
                    keep(
                        s, h, x, nums[0] * a + nums[1] * b, nums[1] * a - nums[0] * b, new, pad
                    )
                return inner

            planes(size_x, plane, 4)
            if not final:
                send_group(s, g, new)
            return carry

        lax.fori_loop(0, groups, sweep, 0)

    each(lambda axis, side: c_copy(axis, side, side).wait_send())

    def finish(g, carry):
        for s in range(SWEEPS - 1):
            each(lambda axis, side, s=s: f_copy(s, g, axis, side, side).wait_send())
        return carry

    lax.fori_loop(0, groups, finish, 0)

    def drain(c, carry):
        core_copy(c).wait_send()
        one_copy(c).wait_send()
        two_copy(c).wait_send()
        for hop in range(RADIX - 1):
            z_send(c, hop, lambda copy: copy.wait_send())
        return carry

    lax.fori_loop(0, steps, drain, 0)


def fast_body(wall_temp, owner_map, stencil_column, material, conductivity, capacity):
    steps, patches, _ = wall_temp.shape
    size_x, size_y, size_z = material.shape
    cells = size_x * size_y
    total = cells * lax.axis_size("sx") * lax.axis_size("sy")
    owner = owner_map[:, 0]
    target = ((owner % 2) * (total // 2) + (owner // 2) * cells + stencil_column)[None, :]
    harms = HARM // lax.axis_size("tm")
    groups = harms // GROUP
    table = dft_table().astype(jnp.float32).reshape(HARM, 2, TIME)[:, :, :steps]
    table = lax.dynamic_slice_in_dim(table, lax.axis_index("tm") * harms, harms, 0)
    f32, bf16 = jnp.float32, jnp.bfloat16
    tile = (size_x, size_y, size_z)
    flat = (cells, size_z)
    padded = (harms, 2, size_x + 2, size_y, size_z)
    x_edge = (SWEEPS - 1, 2, harms, 2, size_y, size_z)
    y_edge = (SWEEPS - 1, 2, harms, 2, size_x, size_z)
    shapes = [
        ((total, patches), bf16),
        ((RING, 4) + flat, f32),
        ((steps, 4) + flat, bf16),
        ((steps, 4) + flat, bf16),
        ((RING, 2) + flat, f32),
        ((steps, 2) + flat, bf16),
        ((steps, 2) + flat, bf16),
        ((RING,) + flat, f32),
        ((steps,) + flat, bf16),
        ((steps,) + flat, bf16),
        ((RADIX * steps,) + flat, bf16),
        (tile, f32),
        (tile, f32),
        ((2, size_x, size_z), f32),
        ((2, size_y, size_z), f32),
        ((2, size_x, size_z), f32),
        ((6,) + tile, f32),
        ((harms,) + tile, f32),
        ((harms,) + tile, f32),
        ((harms, 2) + tile, f32),
        (padded, f32),
        (padded, f32),
        (x_edge, bf16),
        (x_edge, bf16),
        (y_edge, f32),
        (y_edge, f32),
    ]
    sems = (
        [(steps,)] * 6
        + [(2, RADIX - 1, steps)] * 2
        + [(2, 2)] * 2
        + [(SWEEPS - 1, groups, 2)] * 4
    )
    counts = {axis: lax.axis_size(axis) for axis in ("sx", "sy")}
    smem = pl.BlockSpec(memory_space=pltpu.SMEM)
    vmem = pl.BlockSpec(memory_space=pltpu.VMEM)
    return pl.pallas_call(
        functools.partial(blade_kernel, counts),
        out_shape=jax.ShapeDtypeStruct((harms, 2) + tile, f32),
        in_specs=[smem] * 4 + [vmem] * 3,
        out_specs=vmem,
        scratch_shapes=[pltpu.VMEM(*shape) for shape in shapes]
        + [pltpu.SemaphoreType.DMA(shape) for shape in sems],
        compiler_params=pltpu.CompilerParams(
            collective_id=1, has_side_effects=True, vmem_limit_bytes=58 * 1024 * 1024
        ),
    )(
        conductivity,
        capacity,
        table[:, 0].reshape(-1),
        table[:, 1].reshape(-1),
        target,
        wall_temp,
        material,
    )


def solution(mesh):
    in_specs = (
        P("tm", ("sx", "sy"), None),
        P(("sx", "sy"), None),
        P(("sx", "sy")),
        P("sx", "sy", None),
        P(),
        P(),
    )
    out_specs = P("tm", None, "sx", "sy", None)
    direct = mesh.shape["tm"] == RADIX and mesh.shape["sx"] == 2 and mesh.shape["sy"] == 4
    step = fast_body if direct else body
    return jax.shard_map(step, mesh=mesh, in_specs=in_specs, out_specs=out_specs, check_vma=False)
```
